32 devices in a mesh: groups: 2 (over y), seq: 16 (over z, x, core).
Axes of the slice: x: 2, y: 2, z: 4, core: 2. Of those that a mesh axis runs over, the one named last changes fastest.
Arguments:
- features: bfloat16 [4096, 512], P(('groups', 'seq')), parts along dimension 0, may hold values from -6 to 6
- gain_attn: float32 [512], replicated, may hold values from 0.5 to 1.5
- gain_ffn: float32 [512], replicated, may hold values from 0.5 to 1.5
- query_key_value_weight: bfloat16 [512, 1536], replicated, may hold values from -0.5 to 0.5
- w_out: bfloat16 [512, 512], replicated, may hold values from -0.25 to 0.25
- w_in: bfloat16 [512, 2048], replicated, may hold values from -0.25 to 0.25
- w_down: bfloat16 [1024, 512], replicated, may hold values from -0.1875 to 0.1875
- tile_lists: int32 [32, 4], P(('groups', 'seq')), parts along dimension 0, may hold values from 0 to 15, as said below
- tile_count: int32 [32], P(('groups', 'seq')), parts along dimension 0, may hold values from 1 to 4, as said below
- partition: int32 [4096], P(('groups', 'seq')), parts along dimension 0, may hold values from 0 to 31, never falling along the last dimension, each value on 1 to 128 neighbouring positions
- grad_out: bfloat16 [4096, 512], P(('groups', 'seq')), parts along dimension 0, may hold values from -6 to 6
Outputs:
- layer_out: bfloat16 [4096, 512], P(('groups', 'seq')), parts along dimension 0
- d_features: bfloat16 [4096, 512], P(('groups', 'seq')), parts along dimension 0
- grad_qkv: float32 [1024, 1536], P(('groups', 'seq')), parts along dimension 0
- grad_w_out: float32 [1024, 512], P(('groups', 'seq')), parts along dimension 0
- grad_w_in: float32 [1024, 2048], P(('groups', 'seq')), parts along dimension 0
- grad_w_down: float32 [2048, 512], P(('groups', 'seq')), parts along dimension 0
- grad_gains: float32 [2048], P(('groups', 'seq')), parts along dimension 0
The draws below stay inside these ranges and needn't reach their ends.
There are 2 independent parts, one for each index of `groups`. The reference program is written for one: setup_inputs(seed, part) draws one part's arguments, and reference() takes and returns one part's arrays. A program takes and returns all parts, laid end to end along the dimension named above; an argument that names none is the same for every part. Nothing has to cross between parts.
Inputs may be any that keep to these rules, and one draw needn't show every extreme that they name: `tile_lists`: row t holds 4 different tiles, the first of them t. `tile_count`: tile 0 uses all 4 entries. Never falls along the nodes; every partition has 1 to 128 nodes.
All inputs are finite; a program needn't handle non-finite values.
Results may differ from the reference program's by a relative error of at most 0.018.
The reference program's roundings to bfloat16 on the way count: a program that leaves them out, or rounds other values in their place, can miss the bound.
Values may be sent and summed in bfloat16 or wider, within the bound.
A program may use at most 128 MiB of HBM per device.

```python
import math
import jax
import jax.numpy as jnp
import numpy as np
from jax import lax

MODEL_WIDTH = 512
HEADS = 16
HEAD_SIZE = 32
FF = 1024
TOK_DEV = 128
TILE = 128
KT = 4
VN_DEV = 2
NODE_COUNT = 2048
TILES = 16
PARTITION_COUNT = 32


def draw_tile_lists(key, part):
    key = jax.random.fold_in(key, 11)
    row_keys = jax.random.split(key, TILES)

    def pick_tiles(row_key):
        return jax.random.permutation(row_key, TILES - 1)[:KT - 1].astype(jnp.int32)
    others = jax.vmap(pick_tiles)(row_keys)
    own_tile = jnp.arange(TILES, dtype=jnp.int32)
    picked = (own_tile[:, None] + 1 + others) % TILES
    return jnp.concatenate([own_tile[:, None], picked], axis=1).astype(jnp.int32)


def draw_tile_count(key, part):
    key = jax.random.fold_in(key, 23)
    counts = jax.random.randint(key, (TILES,), 1, KT + 1).astype(jnp.int32)
    return counts.at[0].set(KT).astype(jnp.int32)


def levels(stream_key, shape, shards, low, top_value):
    def one(dim, parts):
        steps = jax.random.uniform(jax.random.fold_in(jax.random.fold_in(stream_key, 6), dim), (parts,), jnp.float32, low / len(shards), top_value / len(shards))
        return jnp.repeat(jnp.exp(steps), shape[dim] // parts).reshape((-1,) + (1,) * (len(shape) - dim - 1))

    factor_of = one(*shards[0])
    for cut in shards[1:]:
        factor_of = factor_of * one(*cut)
    return factor_of


def profile(amount, total, most, lean):
    weights = [(1 << 20) // math.isqrt(grade ** lean) + 1 for grade in range(2, amount + 1)]
    spare, holding = total - most - (amount - 1), [1] * (amount - 1)
    while spare > 0:
        free = [i for i in range(amount - 1) if holding[i] < most]
        mass, left = sum([weights[i] for i in free]), spare
        for i in free:
            more = min(most - holding[i], max(1, left * weights[i] // mass), spare)
            holding[i] = holding[i] + more
            spare = spare - more
    return np.array([most] + holding)


def ragged(own_key, count, total, bound, slope):
    if count == 2:
        one = jax.random.randint(own_key, (), max(1, total - bound), min(bound, total - 1) + 1)
        return jnp.stack([one, total - one])
    lengths = jnp.asarray(profile(count, total, bound, slope), jnp.int32)
    couples = (count - 1) // 2
    donor, sink = lengths[1:1 + 2 * couples:2], lengths[2:2 + 2 * couples:2]
    room = jnp.minimum(donor - 1, bound - sink)
    passed = jax.random.randint(jax.random.fold_in(own_key, 1), (couples,), 0, 1 << 20) % (room + 1)
    lengths = lengths.at[1:1 + 2 * couples:2].set(donor - passed).at[2:2 + 2 * couples:2].set(sink + passed)
    return lengths[jax.random.permutation(jax.random.fold_in(own_key, 2), count)]


def scatter_about(stream_key, dims, width, most, shards=(), kind=jnp.bfloat16):
    factor_of = levels(stream_key, dims, shards, -0.22, 0.18) if shards else 1.0
    drawn = jax.random.normal(stream_key, dims, jnp.float32) * width * factor_of
    return jnp.minimum(jnp.maximum(drawn, -most), most).astype(kind)


def setup_inputs(seed: int = 0, part: int = 0) -> dict:
    seeds = jax.random.split(jax.random.key(seed), 12)
    part_splits = jax.random.split(jax.random.fold_in(seeds[11], part), 12)
    return {
        "features": scatter_about(part_splits[0], (NODE_COUNT, MODEL_WIDTH), 1.0, 6.0, ((0, 16),)),
        "gain_attn": jnp.clip(1.0 + 0.1 * jax.random.normal(seeds[1], (MODEL_WIDTH,), jnp.float32), 0.5, 1.5),
        "gain_ffn": jnp.clip(1.0 + 0.1 * jax.random.normal(seeds[2], (MODEL_WIDTH,), jnp.float32), 0.5, 1.5),
        "query_key_value_weight": scatter_about(seeds[3], (MODEL_WIDTH, 3 * MODEL_WIDTH), (MODEL_WIDTH // 4) ** -0.5, 0.5),
        "w_out": scatter_about(seeds[4], (MODEL_WIDTH, MODEL_WIDTH), MODEL_WIDTH ** -0.5, 0.25),
        "w_in": scatter_about(seeds[5], (MODEL_WIDTH, 2 * FF), MODEL_WIDTH ** -0.5, 0.25),
        "w_down": scatter_about(seeds[6], (FF, MODEL_WIDTH), FF ** -0.5, 0.1875),
        "tile_lists": draw_tile_lists(jax.random.fold_in(jax.random.fold_in(seeds[11], part), 71), part),
        "tile_count": draw_tile_count(jax.random.fold_in(jax.random.fold_in(seeds[11], part), 71), part),
        "partition": jnp.searchsorted(jnp.cumsum(ragged(part_splits[9], PARTITION_COUNT, NODE_COUNT, 2 * TOK_DEV // VN_DEV, 1)), jnp.arange(NODE_COUNT), side="right").astype(jnp.int32),
        "grad_out": scatter_about(part_splits[10], (NODE_COUNT, MODEL_WIDTH), 1.0, 6.0, ((0, 16),)),
    }


CAP = 30.0
EPS = 1e-06
HIGH_PRECISION = lax.Precision.HIGHEST

def rms_parts(values):
    inverse = lax.rsqrt(lax.optimization_barrier(jnp.mean(values * values, axis=-1, keepdims=True)) + EPS)
    return (inverse, values * inverse)

def attend_scores(query_rows, key_matrix, virtual_key_rows, active_mask):
    scale = 1.0 / math.sqrt(query_rows.shape[-1])
    query_float = query_rows.astype(jnp.float32)
    near = jnp.einsum('buhe,bmhe->bhum', query_float, key_matrix.astype(jnp.float32)) * scale
    far = jnp.einsum('buhe,phe->bhup', query_float, virtual_key_rows.astype(jnp.float32)) * scale
    near_tanh = jnp.tanh(near / CAP)
    far_tanh = jnp.tanh(far / CAP)
    near_w = jnp.exp(CAP * near_tanh) * active_mask[:, None, None, :]
    far_w = jnp.exp(CAP * far_tanh)
    totals = lax.optimization_barrier(jnp.sum(near_w, axis=-1, keepdims=True)) + lax.optimization_barrier(jnp.sum(far_w, axis=-1, keepdims=True))
    return (near_w / totals, far_w / totals, near_tanh, far_tanh)

def attend_forward(query_rows, key_matrix, value_matrix, virtual_key_rows, virtual_value_rows, active_mask):
    near_p, far_p, near_tanh, far_tanh = attend_scores(query_rows, key_matrix, virtual_key_rows, active_mask)
    near_b = near_p.astype(jnp.bfloat16).astype(jnp.float32)
    far_b = far_p.astype(jnp.bfloat16).astype(jnp.float32)
    output = jnp.einsum('bhum,bmhe->buhe', near_b, value_matrix.astype(jnp.float32))
    output = output + jnp.einsum('bhup,phe->buhe', far_b, virtual_value_rows.astype(jnp.float32))
    return output.astype(jnp.bfloat16)

def attention_backward(query_rows, key_matrix, value_matrix, virtual_key_rows, virtual_value_rows, active_mask, grad_rows):
    near_p, far_p, near_tanh, far_tanh = attend_scores(query_rows, key_matrix, virtual_key_rows, active_mask)
    near_b = near_p.astype(jnp.bfloat16).astype(jnp.float32)
    far_b = far_p.astype(jnp.bfloat16).astype(jnp.float32)
    grad_f = grad_rows.astype(jnp.float32)
    query_float = query_rows.astype(jnp.float32)
    near_dp = jnp.einsum('buhe,bmhe->bhum', grad_f, value_matrix.astype(jnp.float32))
    far_dp = jnp.einsum('buhe,phe->bhup', grad_f, virtual_value_rows.astype(jnp.float32))
    inner = lax.optimization_barrier(jnp.sum(near_p * near_dp, axis=-1, keepdims=True)) + lax.optimization_barrier(jnp.sum(far_p * far_dp, axis=-1, keepdims=True))
    scale = 1.0 / math.sqrt(query_rows.shape[-1])
    near_ds = (near_p * (near_dp - inner) * (1.0 - near_tanh * near_tanh) * scale).astype(jnp.bfloat16).astype(jnp.float32)
    distant_score_gradient = (far_p * (far_dp - inner) * (1.0 - far_tanh * far_tanh) * scale).astype(jnp.bfloat16).astype(jnp.float32)
    query_gradient = jnp.einsum('bhum,bmhe->buhe', near_ds, key_matrix.astype(jnp.float32))
    query_gradient = query_gradient + jnp.einsum('bhup,phe->buhe', distant_score_gradient, virtual_key_rows.astype(jnp.float32))
    key_gradient = jnp.einsum('bhum,buhe->bmhe', near_ds, query_float)
    value_gradient = jnp.einsum('bhum,buhe->bmhe', near_b, grad_f)
    virtual_key_gradient = jnp.einsum('mjsr,msjz->rjz', distant_score_gradient, query_float)
    virtual_value_gradient = jnp.einsum('mjsr,msjz->rjz', far_b, grad_f)
    return (query_gradient, key_gradient, value_gradient, virtual_key_gradient, virtual_value_gradient)

def back_summary(virtual_node_gradient, unit_vn, inverse, counts):
    inner = lax.optimization_barrier(jnp.mean(virtual_node_gradient * unit_vn, axis=-1, keepdims=True))
    return inverse * (virtual_node_gradient - unit_vn * inner) / counts[:, None]

def reference(features, gain_attn, gain_ffn, query_key_value_weight, w_out, w_in, w_down, tile_lists, tile_count, partition, grad_out):
    x_f = features.astype(jnp.float32)
    inv_attn, unit_attn = rms_parts(x_f)
    normed = (unit_attn * gain_attn).astype(jnp.bfloat16)
    totals = jax.ops.segment_sum(normed.astype(jnp.float32), partition, num_segments=PARTITION_COUNT)
    counts = jax.ops.segment_sum(jnp.ones((NODE_COUNT,), jnp.float32), partition, num_segments=PARTITION_COUNT)
    part_mean = totals / counts[:, None]
    inv_vn, unit_vn = rms_parts(part_mean)
    virtual = unit_vn.astype(jnp.bfloat16)
    qkv = jnp.dot(normed, query_key_value_weight, preferred_element_type=jnp.float32).astype(jnp.bfloat16)
    per_head = jnp.transpose(qkv.reshape(NODE_COUNT, 3, HEADS, HEAD_SIZE), (1, 2, 0, 3))
    virt_kv = jnp.dot(virtual, query_key_value_weight[:, MODEL_WIDTH:], preferred_element_type=jnp.float32).astype(jnp.bfloat16)
    virt_head = jnp.transpose(virt_kv.reshape(PARTITION_COUNT, 2, HEADS, HEAD_SIZE), (1, 2, 0, 3))
    live = (jnp.arange(KT, dtype=jnp.int32)[None, :] < tile_count[:, None]).astype(jnp.float32)
    active_mask = jnp.broadcast_to(live[:, :, None], (TILES, KT, TILE)).reshape(TILES, KT * TILE)

    def head_inputs(q_head, k_head, v_head, vk_head, vv_head):
        query_rows = q_head.reshape(TILES, TILE, 1, HEAD_SIZE)
        key_matrix = k_head.reshape(TILES, TILE, HEAD_SIZE)[tile_lists].reshape(TILES, KT * TILE, 1, HEAD_SIZE)
        value_matrix = v_head.reshape(TILES, TILE, HEAD_SIZE)[tile_lists].reshape(TILES, KT * TILE, 1, HEAD_SIZE)
        return (query_rows, key_matrix, value_matrix, vk_head[:, None, :], vv_head[:, None, :])

    def head_forward(operands):
        query_rows, key_matrix, value_matrix, virtual_key_rows, virtual_value_rows = head_inputs(*operands)
        return attend_forward(query_rows, key_matrix, value_matrix, virtual_key_rows, virtual_value_rows, active_mask)
    head_list = (per_head[0], per_head[1], per_head[2], virt_head[0], virt_head[1])
    outs = lax.map(head_forward, head_list)
    attn_out = jnp.transpose(outs.reshape(HEADS, NODE_COUNT, HEAD_SIZE), (1, 0, 2)).reshape(NODE_COUNT, MODEL_WIDTH)
    mixed = jnp.dot(attn_out, w_out, preferred_element_type=jnp.float32)
    resid = (x_f + mixed).astype(jnp.bfloat16)
    res_f = resid.astype(jnp.float32)
    inv_ffn, unit_ffn = rms_parts(res_f)
    normed_ffn = (unit_ffn * gain_ffn).astype(jnp.bfloat16)
    gate_up = jnp.dot(normed_ffn, w_in, preferred_element_type=jnp.float32)
    gate_proj = gate_up[:, :FF]
    up_proj = gate_up[:, FF:]
    sigmoid_gate = jax.nn.sigmoid(gate_proj)
    activated = gate_proj * sigmoid_gate
    hidden = (activated * up_proj).astype(jnp.bfloat16)
    layer_out = (res_f + jnp.dot(hidden, w_down, preferred_element_type=jnp.float32)).astype(jnp.bfloat16)
    d_hidden = jnp.dot(grad_out, w_down.T, preferred_element_type=jnp.float32)
    d_gate = d_hidden * up_proj * sigmoid_gate * (1.0 + gate_proj * (1.0 - sigmoid_gate))
    d_up = d_hidden * activated
    d_both = jnp.concatenate([d_gate, d_up], axis=1).astype(jnp.bfloat16)
    d_normed_ffn = jnp.dot(d_both, w_in.T, preferred_element_type=jnp.float32)
    scaled_ffn = d_normed_ffn * gain_ffn
    d_resid_f = grad_out.astype(jnp.float32) + inv_ffn * (scaled_ffn - unit_ffn * lax.optimization_barrier(jnp.mean(scaled_ffn * unit_ffn, axis=-1, keepdims=True)))
    d_resid = d_resid_f.astype(jnp.bfloat16)
    d_attn = jnp.dot(d_resid, w_out.T, preferred_element_type=jnp.float32).astype(jnp.bfloat16)
    d_heads = jnp.transpose(d_attn.reshape(NODE_COUNT, HEADS, HEAD_SIZE), (1, 0, 2))

    def head_backward(operands):
        query_rows, key_matrix, value_matrix, virtual_key_rows, virtual_value_rows = head_inputs(*operands[:5])
        head_gradient = operands[5].reshape(TILES, TILE, 1, HEAD_SIZE)
        query_gradient, key_gradient, value_gradient, virtual_key_gradient, virtual_value_gradient = attention_backward(query_rows, key_matrix, value_matrix, virtual_key_rows, virtual_value_rows, active_mask, head_gradient)
        kv_pair = jnp.stack([key_gradient.reshape(TILES, KT, TILE, HEAD_SIZE), value_gradient.reshape(TILES, KT, TILE, HEAD_SIZE)], axis=3)
        key_value_gradient = jnp.zeros((TILES, TILE, 2, HEAD_SIZE), jnp.float32).at[tile_lists].add(kv_pair)
        return (query_gradient.astype(jnp.bfloat16).reshape(NODE_COUNT, HEAD_SIZE), key_value_gradient.reshape(NODE_COUNT, 2, HEAD_SIZE), virtual_key_gradient[:, 0, :], virtual_value_gradient[:, 0, :])
    dq_heads, dkv_heads, virtual_key_gradient_heads, dvv_heads = lax.map(head_backward, head_list + (d_heads,))
    query_gradient = jnp.transpose(dq_heads, (1, 0, 2)).reshape(NODE_COUNT, MODEL_WIDTH)
    d_kv = jnp.transpose(dkv_heads, (1, 2, 0, 3)).reshape(NODE_COUNT, 2 * MODEL_WIDTH)
    d_qkv = jnp.concatenate([query_gradient, d_kv.astype(jnp.bfloat16)], axis=1)
    virtual_key_gradient = jnp.transpose(virtual_key_gradient_heads, (1, 0, 2)).reshape(PARTITION_COUNT, MODEL_WIDTH)
    virtual_value_gradient = jnp.transpose(dvv_heads, (1, 0, 2)).reshape(PARTITION_COUNT, MODEL_WIDTH)
    virtual_node_gradient = jnp.dot(virtual_key_gradient, query_key_value_weight[:, MODEL_WIDTH:2 * MODEL_WIDTH].astype(jnp.float32).T, precision=HIGH_PRECISION)
    virtual_node_gradient = virtual_node_gradient + jnp.dot(virtual_value_gradient, query_key_value_weight[:, 2 * MODEL_WIDTH:].astype(jnp.float32).T, precision=HIGH_PRECISION)
    per_part = back_summary(virtual_node_gradient, unit_vn, inv_vn, counts)
    d_normed = jnp.dot(d_qkv, query_key_value_weight.T, preferred_element_type=jnp.float32) + per_part[partition]
    scaled_attn = d_normed * gain_attn
    d_features = (d_resid_f * 0.0 + d_resid.astype(jnp.float32) + inv_attn * (scaled_attn - unit_attn * lax.optimization_barrier(jnp.mean(scaled_attn * unit_attn, axis=-1, keepdims=True)))).astype(jnp.bfloat16)
    virtual_float = virtual.astype(jnp.float32)
    virtual_gradient = jnp.concatenate([jnp.dot(virtual_float.T, virtual_key_gradient, precision=HIGH_PRECISION), jnp.dot(virtual_float.T, virtual_value_gradient, precision=HIGH_PRECISION)], axis=1)
    grad_qkv = jnp.dot(normed.T, d_qkv, preferred_element_type=jnp.float32)
    grad_qkv = grad_qkv + jnp.concatenate([jnp.zeros((MODEL_WIDTH, MODEL_WIDTH), jnp.float32), virtual_gradient], axis=1)
    grad_w_out = jnp.dot(attn_out.T, d_resid, preferred_element_type=jnp.float32)
    grad_w_in = jnp.dot(normed_ffn.T, d_both, preferred_element_type=jnp.float32)
    grad_w_down = jnp.dot(hidden.T, grad_out, preferred_element_type=jnp.float32)
    grad_gains = jnp.concatenate([lax.optimization_barrier(jnp.sum(d_normed * unit_attn, axis=0)), lax.optimization_barrier(jnp.sum(d_normed_ffn * unit_ffn, axis=0))])
    return (layer_out, d_features, grad_qkv, grad_w_out, grad_w_in, grad_w_down, grad_gains)
```

```python
import functools
import math

import jax
import jax.numpy as jnp
from jax import lax
from jax.experimental import pallas as pl
from jax.experimental.pallas import tpu as pltpu
from jax.sharding import PartitionSpec as P

HEADS = 16
KT = 4
VN_DEV = 2
CAP = 30.0
EPS = 1e-06
HIGH_PRECISION = lax.Precision.HIGHEST
VMEM_BYTES = 48 * 1024 * 1024


def rms_parts(values):
    inverse = lax.rsqrt(jnp.mean(values * values, axis=-1, keepdims=True) + EPS)
    return (inverse, values * inverse)


def dot_tn(a, b):
    return lax.dot_general(a, b, (((0,), (0,)), ((), ())), preferred_element_type=jnp.float32)


def dot_nt(a, b):
    return lax.dot_general(a, b, (((1,), (1,)), ((), ())), preferred_element_type=jnp.float32)


def dot_nn(a, b):
    return jnp.dot(a, b, preferred_element_type=jnp.float32)


def tile_weights(lists_ref, qkv_ref, virt_ref, t, head_dim):
    count = lists_ref[t, KT]
    query = qkv_ref[lists_ref[t, 0], 0:head_dim, :]
    scale = 1.0 / (math.sqrt(head_dim) * CAP)
    tanhs, weights = [], []
    for j in range(KT):
        keys = qkv_ref[lists_ref[t, j], head_dim : 2 * head_dim, :]
        th = jnp.tanh(dot_tn(keys, query) * scale)
        w = jnp.exp(CAP * th)
        if j:
            w = w * jnp.where(j < count, 1.0, 0.0)
        tanhs.append(th)
        weights.append(w)
    th = jnp.tanh(dot_tn(virt_ref[0], query) * scale)
    tanhs.append(th)
    weights.append(jnp.exp(CAP * th))
    total = jnp.sum(weights[0], axis=0, keepdims=True)
    for w in weights[1:]:
        total = total + jnp.sum(w, axis=0, keepdims=True)
    inverse = 1.0 / total
    return query, tanhs, [w * inverse for w in weights]


def forward_kernel(head_dim, lists_ref, qkv_ref, virt_ref, out_ref):
    def body(t, carry):
        _, _, probs = tile_weights(lists_ref, qkv_ref, virt_ref, t, head_dim)
        out = dot_nn(virt_ref[1], probs[KT].astype(jnp.bfloat16))
        for j in range(KT):
            values = qkv_ref[lists_ref[t, j], 2 * head_dim : 3 * head_dim, :]
            out = out + dot_nn(values, probs[j].astype(jnp.bfloat16))
        out_ref[t] = out.astype(jnp.bfloat16)
        return carry

    lax.fori_loop(0, out_ref.shape[0], body, 0, unroll=2)


def backward_kernel(
    head_dim, lists_ref, qkv_ref, virt_ref, grad_ref, dq_ref, dkv_ref, dvirt_ref, acc_ref
):
    scale = 1.0 / math.sqrt(head_dim)
    acc_ref[...] = jnp.zeros_like(acc_ref)
    dvirt_ref[...] = jnp.zeros_like(dvirt_ref)

    def body(t, carry):
        query, tanhs, probs = tile_weights(lists_ref, qkv_ref, virt_ref, t, head_dim)
        grad = grad_ref[t]
        dps = []
        for j in range(KT):
            values = qkv_ref[lists_ref[t, j], 2 * head_dim : 3 * head_dim, :]
            dps.append(dot_tn(values, grad))
        dps.append(dot_tn(virt_ref[1], grad))
        inner = jnp.sum(probs[0] * dps[0], axis=0, keepdims=True)
        for j in range(1, KT + 1):
            inner = inner + jnp.sum(probs[j] * dps[j], axis=0, keepdims=True)
        ds = [
            (p * (dp - inner) * (1.0 - th * th) * scale).astype(jnp.bfloat16)
            for p, dp, th in zip(probs, dps, tanhs)
        ]
        pb = [p.astype(jnp.bfloat16) for p in probs]
        dq = dot_nn(virt_ref[0], ds[KT])
        for j in range(KT):
            dq = dq + dot_nn(qkv_ref[lists_ref[t, j], head_dim : 2 * head_dim, :], ds[j])
        dq_ref[t] = dq.astype(jnp.bfloat16)
        for j in range(KT):
            target = lists_ref[t, j]
            acc_ref[target, 0:head_dim, :] += dot_nt(query, ds[j])
            acc_ref[target, head_dim : 2 * head_dim, :] += dot_nt(grad, pb[j])
        dvirt_ref[0:head_dim, :] += dot_nt(query, ds[KT])
        dvirt_ref[head_dim : 2 * head_dim, :] += dot_nt(grad, pb[KT])
        return carry

    lax.fori_loop(0, grad_ref.shape[0], body, 0)
    dkv_ref[...] = acc_ref[...].astype(jnp.bfloat16)


def attention_forward(lists, qkv_all, virt, head_dim):
    tiles_here = lists.shape[0]
    rows = qkv_all.shape[2]
    pairs = tiles_here * rows * (KT * rows + virt.shape[2])
    vmem = pl.BlockSpec(memory_space=pltpu.VMEM)
    return pl.pallas_call(
        functools.partial(forward_kernel, head_dim),
        out_shape=jax.ShapeDtypeStruct((tiles_here, head_dim, rows), jnp.bfloat16),
        in_specs=[pl.BlockSpec(memory_space=pltpu.SMEM), vmem, vmem],
        out_specs=vmem,
        compiler_params=pltpu.CompilerParams(vmem_limit_bytes=VMEM_BYTES),
        cost_estimate=pl.CostEstimate(
            flops=4 * pairs * head_dim, bytes_accessed=2 * qkv_all.size, transcendentals=2 * pairs
        ),
    )(lists, qkv_all, virt)


def attention_backward(lists, qkv_all, virt, grads, head_dim):
    tiles_here, _, rows = grads.shape
    tiles = qkv_all.shape[0]
    parts = virt.shape[2]
    pairs = tiles_here * rows * (KT * rows + parts)
    vmem = pl.BlockSpec(memory_space=pltpu.VMEM)
    return pl.pallas_call(
        functools.partial(backward_kernel, head_dim),
        out_shape=(
            jax.ShapeDtypeStruct((tiles_here, head_dim, rows), jnp.bfloat16),
            jax.ShapeDtypeStruct((tiles, 2 * head_dim, rows), jnp.bfloat16),
            jax.ShapeDtypeStruct((2 * head_dim, parts), jnp.float32),
        ),
        in_specs=[pl.BlockSpec(memory_space=pltpu.SMEM), vmem, vmem, vmem],
        out_specs=(vmem, vmem, vmem),
        scratch_shapes=[pltpu.VMEM((tiles, 2 * head_dim, rows), jnp.float32)],
        compiler_params=pltpu.CompilerParams(vmem_limit_bytes=VMEM_BYTES),
        cost_estimate=pl.CostEstimate(
            flops=10 * pairs * head_dim, bytes_accessed=6 * qkv_all.size, transcendentals=2 * pairs
        ),
    )(lists, qkv_all, virt, grads)


def all_to_all(blocks):
    return lax.all_to_all(blocks, "seq", split_axis=0, concat_axis=0, tiled=True)


def reduce_scatter(blocks):
    size, rows, columns = blocks.shape
    me = lax.axis_index("seq")

    def halve(held, bit):
        mine = (me // bit) % 2
        split = held.reshape(held.shape[0] // 2, 2, rows, columns)
        keep = lax.dynamic_index_in_dim(split, mine, 1, keepdims=False)
        send = lax.dynamic_index_in_dim(split, 1 - mine, 1, keepdims=False)
        got = lax.ppermute(send, "seq", [(i, i ^ bit) for i in range(size)])
        return (keep.astype(jnp.float32) + got.astype(jnp.float32)).astype(jnp.bfloat16)

    held = halve(halve(blocks, 1), 2)
    count = size // 4
    if count > 4:
        groups = [[j + 4 * m for m in range(count)] for j in range(4)]
        got = lax.all_to_all(
            held, "seq", split_axis=0, concat_axis=0, axis_index_groups=groups, tiled=True
        )
        return jnp.sum(got.astype(jnp.float32), axis=0)
    mine = me // 4
    total = lax.dynamic_index_in_dim(held, mine, 0, keepdims=False).astype(jnp.float32)
    for k in range(1, count):
        send = lax.dynamic_index_in_dim(held, (mine + k) % count, 0, keepdims=False)
        perm = [(i, ((i // 4 + k) % count) * 4 + i % 4) for i in range(size)]
        total = total + lax.ppermute(send, "seq", perm).astype(jnp.float32)
    return total


def on_device(
    features,
    gain_attn,
    gain_ffn,
    query_key_value_weight,
    w_out,
    w_in,
    w_down,
    tile_lists,
    tile_count,
    partition,
    grad_out,
):
    rows, width = features.shape
    head_dim = width // HEADS
    hidden_units = w_down.shape[0]
    seq_size = lax.axis_size("seq")
    me = lax.axis_index("seq")
    parts = VN_DEV * seq_size
    slices = seq_size // HEADS
    my_head = me // slices
    my_slice = me % slices
    tiles_here = seq_size // slices
    slice_of_me = me // tiles_here

    x_f = features.astype(jnp.float32)
    inv_attn, unit_attn = rms_parts(x_f)
    normed = (unit_attn * gain_attn).astype(jnp.bfloat16)
    member = (partition[:, None] == jnp.arange(parts, dtype=jnp.int32)[None, :]).astype(
        jnp.bfloat16
    )
    extended = jnp.concatenate([normed, jnp.ones((rows, 128), jnp.bfloat16)], axis=1)
    part_sums = jnp.einsum("rp,rd->pd", member, extended, preferred_element_type=jnp.float32)
    wide = width + 128
    list_row = jnp.concatenate([tile_lists[0], tile_count]).astype(jnp.float32)
    list_row = jnp.pad(list_row, (0, wide - KT - 1))
    first_send = jnp.concatenate(
        [
            part_sums.reshape(seq_size, VN_DEV, wide),
            jnp.broadcast_to(list_row, (seq_size, 1, wide)),
        ],
        axis=1,
    )
    first = all_to_all(first_send)
    own_sums = jnp.sum(first[:, :VN_DEV], axis=0)
    lists_all = first[:, VN_DEV, : KT + 1].astype(jnp.int32)
    second = all_to_all(jnp.broadcast_to(own_sums, (seq_size, VN_DEV, wide)))
    second = second.reshape(parts, wide)
    totals = second[:, :width]
    counts = second[:, width : width + 1]
    part_mean = totals / counts
    inv_vn, unit_vn = rms_parts(part_mean)
    virtual = unit_vn.astype(jnp.bfloat16)

    qkv_t = jnp.einsum(
        "dc,rd->cr", query_key_value_weight, normed, preferred_element_type=jnp.float32
    ).astype(jnp.bfloat16)
    qkv_heads = jnp.transpose(qkv_t.reshape(3, HEADS, head_dim, rows), (1, 0, 2, 3)).reshape(
        HEADS, 1, 3 * head_dim, rows
    )
    qkv_all = all_to_all(
        jnp.broadcast_to(qkv_heads, (HEADS, slices, 3 * head_dim, rows)).reshape(
            seq_size, 3 * head_dim, rows
        )
    )
    lists = lax.dynamic_slice_in_dim(lists_all, my_slice * tiles_here, tiles_here, 0)
    weight_heads = query_key_value_weight.reshape(width, 3, HEADS, head_dim)
    my_columns = lax.dynamic_index_in_dim(weight_heads, my_head, 2, keepdims=False)[:, 1:]
    virt = jnp.einsum(
        "dke,pd->kep", my_columns, virtual, preferred_element_type=jnp.float32
    ).astype(jnp.bfloat16)

    def spread(local):
        if slices == 1:
            return local
        empty = jnp.zeros((seq_size,) + local.shape[1:], local.dtype)
        return lax.dynamic_update_slice_in_dim(empty, local, my_slice * tiles_here, 0)

    def pick_slice(received):
        split = received.reshape((HEADS, slices) + received.shape[1:])
        return lax.dynamic_index_in_dim(split, slice_of_me, 1, keepdims=False)

    out_heads = attention_forward(lists, qkv_all, virt, head_dim)
    attn_out_t = pick_slice(all_to_all(spread(out_heads))).reshape(width, rows)

    mixed = jnp.einsum("dr,de->re", attn_out_t, w_out, preferred_element_type=jnp.float32)
    resid = (x_f + mixed).astype(jnp.bfloat16)
    res_f = resid.astype(jnp.float32)
    inv_ffn, unit_ffn = rms_parts(res_f)
    normed_ffn = (unit_ffn * gain_ffn).astype(jnp.bfloat16)
    gate_up = jnp.dot(normed_ffn, w_in, preferred_element_type=jnp.float32)
    gate_proj = gate_up[:, :hidden_units]
    up_proj = gate_up[:, hidden_units:]
    sigmoid_gate = jax.nn.sigmoid(gate_proj)
    activated = gate_proj * sigmoid_gate
    hidden = (activated * up_proj).astype(jnp.bfloat16)
    layer_out = (res_f + jnp.dot(hidden, w_down, preferred_element_type=jnp.float32)).astype(
        jnp.bfloat16
    )
    d_hidden = jnp.einsum("rd,fd->rf", grad_out, w_down, preferred_element_type=jnp.float32)
    d_gate = d_hidden * up_proj * sigmoid_gate * (1.0 + gate_proj * (1.0 - sigmoid_gate))
    d_up = d_hidden * activated
    d_both = jnp.concatenate([d_gate, d_up], axis=1).astype(jnp.bfloat16)
    d_normed_ffn = jnp.einsum("rf,df->rd", d_both, w_in, preferred_element_type=jnp.float32)
    scaled_ffn = d_normed_ffn * gain_ffn
    d_resid = (
        grad_out.astype(jnp.float32)
        + inv_ffn
        * (scaled_ffn - unit_ffn * jnp.mean(scaled_ffn * unit_ffn, axis=-1, keepdims=True))
    ).astype(jnp.bfloat16)
    d_attn_t = jnp.einsum("de,re->dr", w_out, d_resid, preferred_element_type=jnp.float32).astype(
        jnp.bfloat16
    )
    d_heads = jnp.broadcast_to(
        d_attn_t.reshape(HEADS, 1, head_dim, rows), (HEADS, slices, head_dim, rows)
    ).reshape(seq_size, head_dim, rows)
    grads = lax.dynamic_slice_in_dim(all_to_all(d_heads), my_slice * tiles_here, tiles_here, 0)

    share = width // seq_size
    grad_out_local = jnp.einsum("dr,re->de", attn_out_t, d_resid, preferred_element_type=jnp.float32)
    grad_in_local = jnp.einsum("rd,rf->df", normed_ffn, d_both, preferred_element_type=jnp.float32)
    grad_down_local = jnp.einsum("rf,rd->fd", hidden, grad_out, preferred_element_type=jnp.float32)
    down_blocks = grad_down_local.astype(jnp.bfloat16).reshape(seq_size, -1, share, width)
    early = jnp.concatenate(
        [
            grad_out_local.astype(jnp.bfloat16).reshape(seq_size, share, -1),
            grad_in_local.astype(jnp.bfloat16).reshape(seq_size, share, -1),
        ]
        + [down_blocks[:, i] for i in range(down_blocks.shape[1])],
        axis=2,
    )
    early_sum = reduce_scatter(early)
    grad_w_out = early_sum[:, :width]
    in_end = width + 2 * hidden_units
    grad_w_in = early_sum[:, width:in_end]
    grad_w_down = jnp.concatenate(
        [early_sum[:, c : c + width] for c in range(in_end, early_sum.shape[1], width)], axis=0
    )

    dq, dkv, dvirt = attention_backward(lists, qkv_all, virt, grads, head_dim)
    virt_rows = 2 * head_dim * parts // rows
    back_send = jnp.concatenate(
        [
            spread(dq),
            dkv,
            jnp.broadcast_to(
                dvirt.astype(jnp.bfloat16).reshape(virt_rows, rows), (seq_size, virt_rows, rows)
            ),
        ],
        axis=1,
    )
    back = all_to_all(back_send)
    dq_t = pick_slice(back[:, :head_dim])
    rest = back[:, head_dim:]
    if slices > 1:
        rest = jnp.sum(
            rest.reshape(HEADS, slices, -1, rows).astype(jnp.float32), axis=1
        ).astype(jnp.bfloat16)
    d_qkv_t = jnp.concatenate(
        [dq_t, rest[:, :head_dim], rest[:, head_dim : 2 * head_dim]], axis=0
    ).reshape(3 * width, rows)
    d_virt = (
        rest[:, 2 * head_dim :]
        .reshape(HEADS, 2, head_dim, parts)
        .transpose(1, 0, 2, 3)
        .reshape(2 * width, parts)
    )
    d_virtual = jnp.einsum(
        "sp,ds->pd", d_virt, query_key_value_weight[:, width:], preferred_element_type=jnp.float32
    )
    inner_vn = jnp.mean(d_virtual * unit_vn, axis=-1, keepdims=True)
    per_part = inv_vn * (d_virtual - unit_vn * inner_vn) / counts
    d_normed = jnp.einsum(
        "cr,dc->rd", d_qkv_t, query_key_value_weight, preferred_element_type=jnp.float32
    )
    d_normed = d_normed + jnp.dot(member.astype(jnp.float32), per_part, precision=HIGH_PRECISION)
    scaled_attn = d_normed * gain_attn
    d_features = (
        d_resid.astype(jnp.float32)
        + inv_attn
        * (scaled_attn - unit_attn * jnp.mean(scaled_attn * unit_attn, axis=-1, keepdims=True))
    ).astype(jnp.bfloat16)
    grad_qkv_local = jnp.einsum("rd,cr->dc", normed, d_qkv_t, preferred_element_type=jnp.float32)
    gain_local = jnp.concatenate(
        [jnp.sum(d_normed * unit_attn, axis=0), jnp.sum(d_normed_ffn * unit_ffn, axis=0)]
    )
    gain_share = 2 * width // seq_size
    gain_block = jnp.pad(
        gain_local.astype(jnp.bfloat16).reshape(seq_size, 1, gain_share),
        ((0, 0), (0, share - 1), (0, 128 - gain_share)),
    )
    late = jnp.concatenate(
        [grad_qkv_local.astype(jnp.bfloat16).reshape(seq_size, share, -1), gain_block], axis=2
    )
    late_sum = reduce_scatter(late)
    my_virtual = lax.dynamic_slice_in_dim(virtual, me * share, share, 1)
    virtual_grad = jnp.einsum("pd,sp->ds", my_virtual, d_virt, preferred_element_type=jnp.float32)
    grad_qkv = jnp.concatenate(
        [late_sum[:, :width], late_sum[:, width : 3 * width] + virtual_grad], axis=1
    )
    grad_gains = late_sum[0, 3 * width : 3 * width + gain_share]
    return (layer_out, d_features, grad_qkv, grad_w_out, grad_w_in, grad_w_down, grad_gains)


def solution(mesh):
    node = P(("groups", "seq"), None)
    flat = P(("groups", "seq"))
    return jax.shard_map(
        on_device,
        mesh=mesh,
        in_specs=(node, P(), P(), P(), P(), P(), P(), node, flat, flat, node),
        out_specs=(node, node, node, node, node, node, flat),
        check_vma=False,
    )
```

```python
import functools
import math

import jax
import jax.numpy as jnp
from jax import lax
from jax.experimental import pallas as pl
from jax.experimental.pallas import tpu as pltpu
from jax.sharding import PartitionSpec as P

HEADS = 16
KT = 4
VN_DEV = 2
CAP = 30.0
EPS = 1e-06
HIGH_PRECISION = lax.Precision.HIGHEST
VMEM_BYTES = 48 * 1024 * 1024


def rms_parts(values):
    inverse = lax.rsqrt(jnp.mean(values * values, axis=-1, keepdims=True) + EPS)
    return (inverse, values * inverse)


def dot_tn(a, b):
    return lax.dot_general(a, b, (((0,), (0,)), ((), ())), preferred_element_type=jnp.float32)


def dot_nt(a, b):
    return lax.dot_general(a, b, (((1,), (1,)), ((), ())), preferred_element_type=jnp.float32)


def dot_nn(a, b):
    return jnp.dot(a, b, preferred_element_type=jnp.float32)


def tile_weights(lists_ref, qkv_ref, virt_ref, t, head_dim):
    count = lists_ref[t, KT]
    query = qkv_ref[lists_ref[t, 0], 0:head_dim, :]
    scale = 1.0 / (math.sqrt(head_dim) * CAP)
    tanhs, weights = [], []
    for j in range(KT):
        keys = qkv_ref[lists_ref[t, j], head_dim : 2 * head_dim, :]
        th = jnp.tanh(dot_tn(keys, query) * scale)
        w = jnp.exp(CAP * th)
        if j:
            w = w * jnp.where(j < count, 1.0, 0.0)
        tanhs.append(th)
        weights.append(w)
    th = jnp.tanh(dot_tn(virt_ref[0], query) * scale)
    tanhs.append(th)
    weights.append(jnp.exp(CAP * th))
    total = jnp.sum(weights[0], axis=0, keepdims=True)
    for w in weights[1:]:
        total = total + jnp.sum(w, axis=0, keepdims=True)
    inverse = 1.0 / total
    return query, tanhs, [w * inverse for w in weights]


def forward_kernel(head_dim, lists_ref, qkv_ref, virt_ref, out_ref):
    def body(t, carry):
        _, _, probs = tile_weights(lists_ref, qkv_ref, virt_ref, t, head_dim)
        out = dot_nn(virt_ref[1], probs[KT].astype(jnp.bfloat16))
        for j in range(KT):
            values = qkv_ref[lists_ref[t, j], 2 * head_dim : 3 * head_dim, :]
            out = out + dot_nn(values, probs[j].astype(jnp.bfloat16))
        out_ref[t] = out.astype(jnp.bfloat16)
        return carry

    lax.fori_loop(0, out_ref.shape[0], body, 0, unroll=2)


def backward_kernel(
    head_dim, lists_ref, qkv_ref, virt_ref, grad_ref, dq_ref, dkv_ref, dvirt_ref, acc_ref
):
    scale = 1.0 / math.sqrt(head_dim)
    acc_ref[...] = jnp.zeros_like(acc_ref)
    dvirt_ref[...] = jnp.zeros_like(dvirt_ref)

    def body(t, carry):
        query, tanhs, probs = tile_weights(lists_ref, qkv_ref, virt_ref, t, head_dim)
        grad = grad_ref[t]
        dps = []
        for j in range(KT):
            values = qkv_ref[lists_ref[t, j], 2 * head_dim : 3 * head_dim, :]
            dps.append(dot_tn(values, grad))
        dps.append(dot_tn(virt_ref[1], grad))
        inner = jnp.sum(probs[0] * dps[0], axis=0, keepdims=True)
        for j in range(1, KT + 1):
            inner = inner + jnp.sum(probs[j] * dps[j], axis=0, keepdims=True)
        ds = [
            (p * (dp - inner) * (1.0 - th * th) * scale).astype(jnp.bfloat16)
            for p, dp, th in zip(probs, dps, tanhs)
        ]
        pb = [p.astype(jnp.bfloat16) for p in probs]
        dq = dot_nn(virt_ref[0], ds[KT])
        for j in range(KT):
            dq = dq + dot_nn(qkv_ref[lists_ref[t, j], head_dim : 2 * head_dim, :], ds[j])
        dq_ref[t] = dq.astype(jnp.bfloat16)
        for j in range(KT):
            target = lists_ref[t, j]
            acc_ref[target, 0:head_dim, :] += dot_nt(query, ds[j])
            acc_ref[target, head_dim : 2 * head_dim, :] += dot_nt(grad, pb[j])
        dvirt_ref[0:head_dim, :] += dot_nt(query, ds[KT])
        dvirt_ref[head_dim : 2 * head_dim, :] += dot_nt(grad, pb[KT])
        return carry

    lax.fori_loop(0, grad_ref.shape[0], body, 0)
    dkv_ref[...] = acc_ref[...].astype(jnp.bfloat16)


def attention_forward(lists, qkv_all, virt, head_dim):
    tiles_here = lists.shape[0]
    rows = qkv_all.shape[2]
    pairs = tiles_here * rows * (KT * rows + virt.shape[2])
    vmem = pl.BlockSpec(memory_space=pltpu.VMEM)
    return pl.pallas_call(
        functools.partial(forward_kernel, head_dim),
        out_shape=jax.ShapeDtypeStruct((tiles_here, head_dim, rows), jnp.bfloat16),
        in_specs=[pl.BlockSpec(memory_space=pltpu.SMEM), vmem, vmem],
        out_specs=vmem,
        compiler_params=pltpu.CompilerParams(vmem_limit_bytes=VMEM_BYTES),
        cost_estimate=pl.CostEstimate(
            flops=4 * pairs * head_dim, bytes_accessed=2 * qkv_all.size, transcendentals=2 * pairs
        ),
    )(lists, qkv_all, virt)


def attention_backward(lists, qkv_all, virt, grads, head_dim):
    tiles_here, _, rows = grads.shape
    tiles = qkv_all.shape[0]
    parts = virt.shape[2]
    pairs = tiles_here * rows * (KT * rows + parts)
    vmem = pl.BlockSpec(memory_space=pltpu.VMEM)
    return pl.pallas_call(
        functools.partial(backward_kernel, head_dim),
        out_shape=(
            jax.ShapeDtypeStruct((tiles_here, head_dim, rows), jnp.bfloat16),
            jax.ShapeDtypeStruct((tiles, 2 * head_dim, rows), jnp.bfloat16),
            jax.ShapeDtypeStruct((2 * head_dim, parts), jnp.float32),
        ),
        in_specs=[pl.BlockSpec(memory_space=pltpu.SMEM), vmem, vmem, vmem],
        out_specs=(vmem, vmem, vmem),
        scratch_shapes=[pltpu.VMEM((tiles, 2 * head_dim, rows), jnp.float32)],
        compiler_params=pltpu.CompilerParams(vmem_limit_bytes=VMEM_BYTES),
        cost_estimate=pl.CostEstimate(
            flops=10 * pairs * head_dim, bytes_accessed=6 * qkv_all.size, transcendentals=2 * pairs
        ),
    )(lists, qkv_all, virt, grads)


def all_to_all(blocks):
    return lax.all_to_all(blocks, "seq", split_axis=0, concat_axis=0, tiled=True)


def halve(held, bit):
    size = lax.axis_size("seq")
    mine = (lax.axis_index("seq") // bit) % 2
    split = held.reshape((held.shape[0] // 2, 2) + held.shape[1:])
    keep = lax.dynamic_index_in_dim(split, mine, 1, keepdims=False)
    send = lax.dynamic_index_in_dim(split, 1 - mine, 1, keepdims=False)
    got = lax.ppermute(send, "seq", [(i, i ^ bit) for i in range(size)])
    return (keep.astype(jnp.float32) + got.astype(jnp.float32)).astype(jnp.bfloat16)


def finish(held):
    size = lax.axis_size("seq")
    count = size // 4
    if count > 4:
        groups = [[j + 4 * m for m in range(count)] for j in range(4)]
        got = lax.all_to_all(
            held, "seq", split_axis=0, concat_axis=0, axis_index_groups=groups, tiled=True
        )
        return jnp.sum(got.astype(jnp.float32), axis=0)
    mine = lax.axis_index("seq") // 4
    total = lax.dynamic_index_in_dim(held, mine, 0, keepdims=False).astype(jnp.float32)
    for k in range(1, count):
        send = lax.dynamic_index_in_dim(held, (mine + k) % count, 0, keepdims=False)
        perm = [(i, ((i // 4 + k) % count) * 4 + i % 4) for i in range(size)]
        total = total + lax.ppermute(send, "seq", perm).astype(jnp.float32)
    return total


def on_device(
    features,
    gain_attn,
    gain_ffn,
    query_key_value_weight,
    w_out,
    w_in,
    w_down,
    tile_lists,
    tile_count,
    partition,
    grad_out,
):
    rows, width = features.shape
    head_dim = width // HEADS
    hidden_units = w_down.shape[0]
    seq_size = lax.axis_size("seq")
    me = lax.axis_index("seq")
    parts = VN_DEV * seq_size
    slices = seq_size // HEADS
    my_head = me // slices
    my_slice = me % slices
    tiles_here = seq_size // slices
    slice_of_me = me // tiles_here

    x_f = features.astype(jnp.float32)
    inv_attn, unit_attn = rms_parts(x_f)
    normed = (unit_attn * gain_attn).astype(jnp.bfloat16)
    member = (partition[:, None] == jnp.arange(parts, dtype=jnp.int32)[None, :]).astype(
        jnp.bfloat16
    )
    extended = jnp.concatenate([normed, jnp.ones((rows, 128), jnp.bfloat16)], axis=1)
    part_sums = jnp.einsum("rp,rd->pd", member, extended, preferred_element_type=jnp.float32)
    wide = width + 128
    list_row = jnp.concatenate([tile_lists[0], tile_count]).astype(jnp.float32)
    list_row = jnp.pad(list_row, (0, wide - KT - 1))
    first_send = jnp.concatenate(
        [
            part_sums.reshape(seq_size, VN_DEV, wide),
            jnp.broadcast_to(list_row, (seq_size, 1, wide)),
        ],
        axis=1,
    )
    first = all_to_all(first_send)
    own_sums = jnp.sum(first[:, :VN_DEV], axis=0)
    lists_all = first[:, VN_DEV, : KT + 1].astype(jnp.int32)
    second = all_to_all(jnp.broadcast_to(own_sums, (seq_size, VN_DEV, wide)))
    second = second.reshape(parts, wide)
    totals = second[:, :width]
    counts = second[:, width : width + 1]
    part_mean = totals / counts
    inv_vn, unit_vn = rms_parts(part_mean)
    virtual = unit_vn.astype(jnp.bfloat16)

    qkv_t = jnp.einsum(
        "dc,rd->cr", query_key_value_weight, normed, preferred_element_type=jnp.float32
    ).astype(jnp.bfloat16)
    qkv_heads = jnp.transpose(qkv_t.reshape(3, HEADS, head_dim, rows), (1, 0, 2, 3)).reshape(
        HEADS, 1, 3 * head_dim, rows
    )
    qkv_all = all_to_all(
        jnp.broadcast_to(qkv_heads, (HEADS, slices, 3 * head_dim, rows)).reshape(
            seq_size, 3 * head_dim, rows
        )
    )
    lists = lax.dynamic_slice_in_dim(lists_all, my_slice * tiles_here, tiles_here, 0)
    weight_heads = query_key_value_weight.reshape(width, 3, HEADS, head_dim)
    my_columns = lax.dynamic_index_in_dim(weight_heads, my_head, 2, keepdims=False)[:, 1:]
    virt = jnp.einsum(
        "dke,pd->kep", my_columns, virtual, preferred_element_type=jnp.float32
    ).astype(jnp.bfloat16)

    def spread(local):
        if slices == 1:
            return local
        empty = jnp.zeros((seq_size,) + local.shape[1:], local.dtype)
        return lax.dynamic_update_slice_in_dim(empty, local, my_slice * tiles_here, 0)

    def pick_slice(received):
        split = received.reshape((HEADS, slices) + received.shape[1:])
        return lax.dynamic_index_in_dim(split, slice_of_me, 1, keepdims=False)

    out_heads = attention_forward(lists, qkv_all, virt, head_dim)
    attn_out_t = pick_slice(all_to_all(spread(out_heads))).reshape(width, rows)

    mixed = jnp.einsum("dr,de->re", attn_out_t, w_out, preferred_element_type=jnp.float32)
    resid = (x_f + mixed).astype(jnp.bfloat16)
    res_f = resid.astype(jnp.float32)
    inv_ffn, unit_ffn = rms_parts(res_f)
    normed_ffn = (unit_ffn * gain_ffn).astype(jnp.bfloat16)
    gate_up = jnp.dot(normed_ffn, w_in, preferred_element_type=jnp.float32)
    gate_proj = gate_up[:, :hidden_units]
    up_proj = gate_up[:, hidden_units:]
    sigmoid_gate = jax.nn.sigmoid(gate_proj)
    activated = gate_proj * sigmoid_gate
    hidden = (activated * up_proj).astype(jnp.bfloat16)
    layer_out = (res_f + jnp.dot(hidden, w_down, preferred_element_type=jnp.float32)).astype(
        jnp.bfloat16
    )
    d_hidden = jnp.einsum("rd,fd->rf", grad_out, w_down, preferred_element_type=jnp.float32)
    d_gate = d_hidden * up_proj * sigmoid_gate * (1.0 + gate_proj * (1.0 - sigmoid_gate))
    d_up = d_hidden * activated
    d_both = jnp.concatenate([d_gate, d_up], axis=1).astype(jnp.bfloat16)
    d_normed_ffn = jnp.einsum("rf,df->rd", d_both, w_in, preferred_element_type=jnp.float32)
    scaled_ffn = d_normed_ffn * gain_ffn
    d_resid = (
        grad_out.astype(jnp.float32)
        + inv_ffn
        * (scaled_ffn - unit_ffn * jnp.mean(scaled_ffn * unit_ffn, axis=-1, keepdims=True))
    ).astype(jnp.bfloat16)
    d_attn_t = jnp.einsum("de,re->dr", w_out, d_resid, preferred_element_type=jnp.float32).astype(
        jnp.bfloat16
    )
    d_heads = jnp.broadcast_to(
        d_attn_t.reshape(HEADS, 1, head_dim, rows), (HEADS, slices, head_dim, rows)
    ).reshape(seq_size, head_dim, rows)
    grads = lax.dynamic_slice_in_dim(all_to_all(d_heads), my_slice * tiles_here, tiles_here, 0)

    share = width // seq_size
    grad_out_local = jnp.einsum("dr,re->de", attn_out_t, d_resid, preferred_element_type=jnp.float32)
    grad_in_local = jnp.einsum("rd,rf->df", normed_ffn, d_both, preferred_element_type=jnp.float32)
    grad_down_local = jnp.einsum("rf,rd->fd", hidden, grad_out, preferred_element_type=jnp.float32)
    down_blocks = grad_down_local.astype(jnp.bfloat16).reshape(seq_size, -1, share, width)
    early = jnp.concatenate(
        [
            grad_out_local.astype(jnp.bfloat16).reshape(seq_size, share, -1),
            grad_in_local.astype(jnp.bfloat16).reshape(seq_size, share, -1),
        ]
        + [down_blocks[:, i] for i in range(down_blocks.shape[1])],
        axis=2,
    )
    early = halve(early, 1)
    grads, early = lax.optimization_barrier((grads, early))
    early = halve(early, 2)

    dq, dkv, dvirt = attention_backward(lists, qkv_all, virt, grads, head_dim)
    dq, early = lax.optimization_barrier((dq, early))
    early_sum = finish(early)
    virt_rows = 2 * head_dim * parts // rows
    back_send = jnp.concatenate(
        [
            spread(dq),
            dkv,
            jnp.broadcast_to(
                dvirt.astype(jnp.bfloat16).reshape(virt_rows, rows), (seq_size, virt_rows, rows)
            ),
        ],
        axis=1,
    )
    back = all_to_all(back_send)
    back, early_sum = lax.optimization_barrier((back, early_sum))
    dq_t = pick_slice(back[:, :head_dim])
    rest = back[:, head_dim:]
    if slices > 1:
        rest = jnp.sum(
            rest.reshape(HEADS, slices, -1, rows).astype(jnp.float32), axis=1
        ).astype(jnp.bfloat16)
    d_qkv_t = jnp.concatenate(
        [dq_t, rest[:, :head_dim], rest[:, head_dim : 2 * head_dim]], axis=0
    ).reshape(3 * width, rows)
    d_virt = (
        rest[:, 2 * head_dim :]
        .reshape(HEADS, 2, head_dim, parts)
        .transpose(1, 0, 2, 3)
        .reshape(2 * width, parts)
    )
    d_virtual = jnp.einsum(
        "sp,ds->pd", d_virt, query_key_value_weight[:, width:], preferred_element_type=jnp.float32
    )
    inner_vn = jnp.mean(d_virtual * unit_vn, axis=-1, keepdims=True)
    per_part = inv_vn * (d_virtual - unit_vn * inner_vn) / counts
    d_normed = jnp.einsum(
        "cr,dc->rd", d_qkv_t, query_key_value_weight, preferred_element_type=jnp.float32
    )
    d_normed = d_normed + jnp.dot(member.astype(jnp.float32), per_part, precision=HIGH_PRECISION)
    scaled_attn = d_normed * gain_attn
    d_features = (
        d_resid.astype(jnp.float32)
        + inv_attn
        * (scaled_attn - unit_attn * jnp.mean(scaled_attn * unit_attn, axis=-1, keepdims=True))
    ).astype(jnp.bfloat16)
    grad_qkv_local = jnp.einsum("rd,cr->dc", normed, d_qkv_t, preferred_element_type=jnp.float32)
    gain_local = jnp.concatenate(
        [jnp.sum(d_normed * unit_attn, axis=0), jnp.sum(d_normed_ffn * unit_ffn, axis=0)]
    )
    gain_share = 2 * width // seq_size
    gain_block = jnp.pad(
        gain_local.astype(jnp.bfloat16).reshape(seq_size, 1, gain_share),
        ((0, 0), (0, share - 1), (0, 128 - gain_share)),
    )
    late = jnp.concatenate(
        [grad_qkv_local.astype(jnp.bfloat16).reshape(seq_size, share, -1), gain_block], axis=2
    )
    late_sum = finish(halve(halve(late, 1), 2))
    grad_w_out = early_sum[:, :width]
    in_end = width + 2 * hidden_units
    grad_w_in = early_sum[:, width:in_end]
    grad_w_down = jnp.concatenate(
        [early_sum[:, c : c + width] for c in range(in_end, early_sum.shape[1], width)], axis=0
    )
    my_virtual = lax.dynamic_slice_in_dim(virtual, me * share, share, 1)
    virtual_grad = jnp.einsum("pd,sp->ds", my_virtual, d_virt, preferred_element_type=jnp.float32)
    grad_qkv = jnp.concatenate(
        [late_sum[:, :width], late_sum[:, width : 3 * width] + virtual_grad], axis=1
    )
    grad_gains = late_sum[0, 3 * width : 3 * width + gain_share]
    return (layer_out, d_features, grad_qkv, grad_w_out, grad_w_in, grad_w_down, grad_gains)


def solution(mesh):
    node = P(("groups", "seq"), None)
    flat = P(("groups", "seq"))
    return jax.shard_map(
        on_device,
        mesh=mesh,
        in_specs=(node, P(), P(), P(), P(), P(), P(), node, flat, flat, node),
        out_specs=(node, node, node, node, node, node, flat),
        check_vma=False,
    )
```

```python
import functools
import math

import jax
import jax.numpy as jnp
from jax import lax
from jax.experimental import pallas as pl
from jax.experimental.pallas import tpu as pltpu
from jax.sharding import PartitionSpec as P

HEADS = 16
KT = 4
VN_DEV = 2
CAP = 30.0
EPS = 1e-06
HIGH_PRECISION = lax.Precision.HIGHEST
VMEM_BYTES = 48 * 1024 * 1024


def rms_parts(values):
    inverse = lax.rsqrt(jnp.mean(values * values, axis=-1, keepdims=True) + EPS)
    return (inverse, values * inverse)


def dot_tn(a, b):
    return lax.dot_general(a, b, (((0,), (0,)), ((), ())), preferred_element_type=jnp.float32)


def dot_nt(a, b):
    return lax.dot_general(a, b, (((1,), (1,)), ((), ())), preferred_element_type=jnp.float32)


def dot_nn(a, b):
    return jnp.dot(a, b, preferred_element_type=jnp.float32)


def tile_weights(lists_ref, qkv_ref, virt_ref, t, head_dim):
    count = lists_ref[t, KT]
    query = qkv_ref[lists_ref[t, 0], 0:head_dim, :]
    scale = 1.0 / (math.sqrt(head_dim) * CAP)
    tanhs, weights = [], []
    for j in range(KT):
        keys = qkv_ref[lists_ref[t, j], head_dim : 2 * head_dim, :]
        th = jnp.tanh(dot_tn(keys, query) * scale)
        w = jnp.exp(CAP * th)
        if j:
            w = w * jnp.where(j < count, 1.0, 0.0)
        tanhs.append(th)
        weights.append(w)
    th = jnp.tanh(dot_tn(virt_ref[0], query) * scale)
    tanhs.append(th)
    weights.append(jnp.exp(CAP * th))
    total = jnp.sum(weights[0], axis=0, keepdims=True)
    for w in weights[1:]:
        total = total + jnp.sum(w, axis=0, keepdims=True)
    inverse = 1.0 / total
    return query, tanhs, [w * inverse for w in weights]


def forward_kernel(head_dim, lists_ref, qkv_ref, virt_ref, out_ref):
    def body(t, carry):
        _, _, probs = tile_weights(lists_ref, qkv_ref, virt_ref, t, head_dim)
        out = dot_nn(virt_ref[1], probs[KT].astype(jnp.bfloat16))
        for j in range(KT):
            values = qkv_ref[lists_ref[t, j], 2 * head_dim : 3 * head_dim, :]
            out = out + dot_nn(values, probs[j].astype(jnp.bfloat16))
        out_ref[t] = out.astype(jnp.bfloat16)
        return carry

    lax.fori_loop(0, out_ref.shape[0], body, 0, unroll=2)


def backward_kernel(
    head_dim, lists_ref, qkv_ref, virt_ref, grad_ref, dq_ref, dkv_ref, dvirt_ref, acc_ref
):
    scale = 1.0 / math.sqrt(head_dim)
    acc_ref[...] = jnp.zeros_like(acc_ref)
    dvirt_ref[...] = jnp.zeros_like(dvirt_ref)

    def body(t, carry):
        query, tanhs, probs = tile_weights(lists_ref, qkv_ref, virt_ref, t, head_dim)
        grad = grad_ref[t]
        dps = []
        for j in range(KT):
            values = qkv_ref[lists_ref[t, j], 2 * head_dim : 3 * head_dim, :]
            dps.append(dot_tn(values, grad))
        dps.append(dot_tn(virt_ref[1], grad))
        inner = jnp.sum(probs[0] * dps[0], axis=0, keepdims=True)
        for j in range(1, KT + 1):
            inner = inner + jnp.sum(probs[j] * dps[j], axis=0, keepdims=True)
        ds = [
            (p * (dp - inner) * (1.0 - th * th) * scale).astype(jnp.bfloat16)
            for p, dp, th in zip(probs, dps, tanhs)
        ]
        pb = [p.astype(jnp.bfloat16) for p in probs]
        dq = dot_nn(virt_ref[0], ds[KT])
        for j in range(KT):
            dq = dq + dot_nn(qkv_ref[lists_ref[t, j], head_dim : 2 * head_dim, :], ds[j])
        dq_ref[t] = dq.astype(jnp.bfloat16)
        for j in range(KT):
            target = lists_ref[t, j]
            acc_ref[target, 0:head_dim, :] += dot_nt(query, ds[j])
            acc_ref[target, head_dim : 2 * head_dim, :] += dot_nt(grad, pb[j])
        dvirt_ref[0:head_dim, :] += dot_nt(query, ds[KT])
        dvirt_ref[head_dim : 2 * head_dim, :] += dot_nt(grad, pb[KT])
        return carry

    lax.fori_loop(0, grad_ref.shape[0], body, 0)
    dkv_ref[...] = acc_ref[...].astype(jnp.bfloat16)


def attention_forward(lists, qkv_all, virt, head_dim):
    tiles_here = lists.shape[0]
    rows = qkv_all.shape[2]
    pairs = tiles_here * rows * (KT * rows + virt.shape[2])
    vmem = pl.BlockSpec(memory_space=pltpu.VMEM)
    return pl.pallas_call(
        functools.partial(forward_kernel, head_dim),
        out_shape=jax.ShapeDtypeStruct((tiles_here, head_dim, rows), jnp.bfloat16),
        in_specs=[pl.BlockSpec(memory_space=pltpu.SMEM), vmem, vmem],
        out_specs=vmem,
        compiler_params=pltpu.CompilerParams(vmem_limit_bytes=VMEM_BYTES),
        cost_estimate=pl.CostEstimate(
            flops=4 * pairs * head_dim, bytes_accessed=2 * qkv_all.size, transcendentals=2 * pairs
        ),
    )(lists, qkv_all, virt)


def attention_backward(lists, qkv_all, virt, grads, head_dim):
    tiles_here, _, rows = grads.shape
    tiles = qkv_all.shape[0]
    parts = virt.shape[2]
    pairs = tiles_here * rows * (KT * rows + parts)
    vmem = pl.BlockSpec(memory_space=pltpu.VMEM)
    return pl.pallas_call(
        functools.partial(backward_kernel, head_dim),
        out_shape=(
            jax.ShapeDtypeStruct((tiles_here, head_dim, rows), jnp.bfloat16),
            jax.ShapeDtypeStruct((tiles, 2 * head_dim, rows), jnp.bfloat16),
            jax.ShapeDtypeStruct((2 * head_dim, parts), jnp.float32),
        ),
        in_specs=[pl.BlockSpec(memory_space=pltpu.SMEM), vmem, vmem, vmem],
        out_specs=(vmem, vmem, vmem),
        scratch_shapes=[pltpu.VMEM((tiles, 2 * head_dim, rows), jnp.float32)],
        compiler_params=pltpu.CompilerParams(vmem_limit_bytes=VMEM_BYTES),
        cost_estimate=pl.CostEstimate(
            flops=10 * pairs * head_dim, bytes_accessed=6 * qkv_all.size, transcendentals=2 * pairs
        ),
    )(lists, qkv_all, virt, grads)


def all_to_all(blocks):
    return lax.all_to_all(blocks, "seq", split_axis=0, concat_axis=0, tiled=True)


def as_bits(blocks):
    bits = blocks.shape[0].bit_length() - 1
    return blocks.reshape((2,) * bits + blocks.shape[1:]), list(range(bits - 1, -1, -1))


def halve(held, left, bit, last=False):
    size = lax.axis_size("seq")
    mine = (lax.axis_index("seq") // (1 << bit)) % 2
    axis = left.index(bit)
    keep = lax.dynamic_index_in_dim(held, mine, axis, keepdims=False)
    send = lax.dynamic_index_in_dim(held, 1 - mine, axis, keepdims=False)
    got = lax.ppermute(send, "seq", [(i, i ^ (1 << bit)) for i in range(size)])
    total = keep.astype(jnp.float32) + got.astype(jnp.float32)
    rest = [b for b in left if b != bit]
    return (total if not rest else total.astype(jnp.bfloat16)), rest


def reduce_in_order(blocks, order):
    held, left = as_bits(blocks)
    for bit in order:
        held, left = halve(held, left, bit)
    return held


def exchange_kernel(
    slices, sums_ref, list_ref, qkv_ref, qkv_all_ref, second_ref, first_ref, own_ref, send, recv
):
    size = qkv_all_ref.shape[0]
    me = lax.axis_index("seq")

    def peer(k):
        return lax.rem(me + k, size)

    def each(step):
        def body(k, carry):
            step(k, peer(k))
            return carry

        lax.fori_loop(1, size, body, 0)

    def remote(src, dst, which, k, to):
        return pltpu.make_async_remote_copy(
            src_ref=src,
            dst_ref=dst,
            send_sem=send.at[which, k],
            recv_sem=recv.at[which, k],
            device_id={"seq": to},
            device_id_type=pl.DeviceIdType.MESH,
        )

    def first_copy(k, to):
        return remote(sums_ref.at[to], first_ref.at[me], 0, k, to)

    def second_copy(k, to):
        return remote(own_ref, second_ref.at[me], 1, k, to)

    def head_copy(k, to):
        return remote(qkv_ref.at[to // slices], qkv_all_ref.at[me], 2, k, to)

    barrier = pltpu.get_barrier_semaphore()
    each(
        lambda k, to: pl.semaphore_signal(
            barrier, inc=1, device_id={"seq": to}, device_id_type=pl.DeviceIdType.MESH
        )
    )
    first_ref[me] = sums_ref[me]
    qkv_all_ref[me] = qkv_ref[me // slices]
    pl.semaphore_wait(barrier, size - 1)
    each(lambda k, to: first_copy(k, to).start())
    each(lambda k, to: head_copy(k, to).start())
    each(lambda k, to: first_copy(k, to).wait_recv())
    own_ref[...] = list_ref[...] + jnp.sum(first_ref[...], axis=0)
    each(lambda k, to: second_copy(k, to).start())
    second_ref[me] = own_ref[...]
    each(lambda k, to: second_copy(k, to).wait_recv())
    each(lambda k, to: head_copy(k, to).wait_recv())
    each(lambda k, to: first_copy(k, to).wait_send())
    each(lambda k, to: second_copy(k, to).wait_send())
    each(lambda k, to: head_copy(k, to).wait_send())


def exchange(sums, list_rows, qkv_heads, slices):
    size = sums.shape[0]
    vmem = pl.BlockSpec(memory_space=pltpu.VMEM)
    return pl.pallas_call(
        functools.partial(exchange_kernel, slices),
        out_shape=(
            jax.ShapeDtypeStruct((size,) + qkv_heads.shape[1:], qkv_heads.dtype),
            jax.ShapeDtypeStruct(sums.shape, sums.dtype),
        ),
        in_specs=[vmem, vmem, vmem],
        out_specs=(vmem, vmem),
        scratch_shapes=[
            pltpu.VMEM(sums.shape, sums.dtype),
            pltpu.VMEM(sums.shape[1:], sums.dtype),
            pltpu.SemaphoreType.DMA((3, size)),
            pltpu.SemaphoreType.DMA((3, size)),
        ],
        compiler_params=pltpu.CompilerParams(
            vmem_limit_bytes=VMEM_BYTES, collective_id=0, has_side_effects=True
        ),
        cost_estimate=pl.CostEstimate(
            flops=sums.size, bytes_accessed=4 * size * qkv_heads[0].size, transcendentals=0
        ),
    )(sums, list_rows, qkv_heads)


def on_device(
    features,
    gain_attn,
    gain_ffn,
    query_key_value_weight,
    w_out,
    w_in,
    w_down,
    tile_lists,
    tile_count,
    partition,
    grad_out,
):
    rows, width = features.shape
    head_dim = width // HEADS
    hidden_units = w_down.shape[0]
    seq_size = lax.axis_size("seq")
    me = lax.axis_index("seq")
    parts = VN_DEV * seq_size
    slices = seq_size // HEADS
    my_head = me // slices
    my_slice = me % slices
    tiles_here = seq_size // slices
    slice_of_me = me // tiles_here

    x_f = features.astype(jnp.float32)
    inv_attn, unit_attn = rms_parts(x_f)
    normed = (unit_attn * gain_attn).astype(jnp.bfloat16)
    member = (partition[:, None] == jnp.arange(parts, dtype=jnp.int32)[None, :]).astype(
        jnp.bfloat16
    )
    part_sums = jnp.einsum("rp,rd->pd", member, normed, preferred_element_type=jnp.float32)
    part_counts = jnp.sum(member.astype(jnp.float32), axis=0)
    lanes = 128
    sum_rows = VN_DEV * width // lanes
    list_at = sum_rows + VN_DEV
    block_rows = -(-(list_at + 1) // 8) * 8
    sums = jnp.concatenate(
        [
            part_sums.reshape(seq_size, sum_rows, lanes),
            jnp.broadcast_to(
                part_counts.reshape(seq_size, VN_DEV, 1), (seq_size, VN_DEV, lanes)
            ),
            jnp.zeros((seq_size, block_rows - list_at, lanes), jnp.float32),
        ],
        axis=1,
    )
    list_rows = jnp.pad(
        jnp.concatenate([tile_lists[0], tile_count]).astype(jnp.float32)[None],
        ((list_at, block_rows - list_at - 1), (0, lanes - KT - 1)),
    )
    qkv_t = jnp.einsum(
        "dc,rd->cr", query_key_value_weight, normed, preferred_element_type=jnp.float32
    ).astype(jnp.bfloat16)
    qkv_heads = jnp.transpose(qkv_t.reshape(3, HEADS, head_dim, rows), (1, 0, 2, 3)).reshape(
        HEADS, 3 * head_dim, rows
    )
    qkv_all, second = exchange(sums, list_rows, qkv_heads, slices)
    totals = second[:, :sum_rows].reshape(parts, width)
    counts = second[:, sum_rows:list_at, :1].reshape(parts, 1)
    lists_all = second[:, list_at, : KT + 1].astype(jnp.int32)
    part_mean = totals / counts
    inv_vn, unit_vn = rms_parts(part_mean)
    virtual = unit_vn.astype(jnp.bfloat16)

    lists = lax.dynamic_slice_in_dim(lists_all, my_slice * tiles_here, tiles_here, 0)
    weight_heads = query_key_value_weight.reshape(width, 3, HEADS, head_dim)
    my_columns = lax.dynamic_index_in_dim(weight_heads, my_head, 2, keepdims=False)[:, 1:]
    virt = jnp.einsum(
        "dke,pd->kep", my_columns, virtual, preferred_element_type=jnp.float32
    ).astype(jnp.bfloat16)

    def spread(local):
        if slices == 1:
            return local
        empty = jnp.zeros((seq_size,) + local.shape[1:], local.dtype)
        return lax.dynamic_update_slice_in_dim(empty, local, my_slice * tiles_here, 0)

    def pick_slice(received):
        split = received.reshape((HEADS, slices) + received.shape[1:])
        return lax.dynamic_index_in_dim(split, slice_of_me, 1, keepdims=False)

    out_heads = attention_forward(lists, qkv_all, virt, head_dim)
    attn_out_t = pick_slice(all_to_all(spread(out_heads))).reshape(width, rows)

    mixed = jnp.einsum("dr,de->re", attn_out_t, w_out, preferred_element_type=jnp.float32)
    resid = (x_f + mixed).astype(jnp.bfloat16)
    res_f = resid.astype(jnp.float32)
    inv_ffn, unit_ffn = rms_parts(res_f)
    normed_ffn = (unit_ffn * gain_ffn).astype(jnp.bfloat16)
    gate_up = jnp.dot(normed_ffn, w_in, preferred_element_type=jnp.float32)
    gate_proj = gate_up[:, :hidden_units]
    up_proj = gate_up[:, hidden_units:]
    sigmoid_gate = jax.nn.sigmoid(gate_proj)
    activated = gate_proj * sigmoid_gate
    hidden = (activated * up_proj).astype(jnp.bfloat16)
    layer_out = (res_f + jnp.dot(hidden, w_down, preferred_element_type=jnp.float32)).astype(
        jnp.bfloat16
    )
    d_hidden = jnp.einsum("rd,fd->rf", grad_out, w_down, preferred_element_type=jnp.float32)
    d_gate = d_hidden * up_proj * sigmoid_gate * (1.0 + gate_proj * (1.0 - sigmoid_gate))
    d_up = d_hidden * activated
    d_both = jnp.concatenate([d_gate, d_up], axis=1).astype(jnp.bfloat16)
    d_normed_ffn = jnp.einsum("rf,df->rd", d_both, w_in, preferred_element_type=jnp.float32)
    scaled_ffn = d_normed_ffn * gain_ffn
    d_resid = (
        grad_out.astype(jnp.float32)
        + inv_ffn
        * (scaled_ffn - unit_ffn * jnp.mean(scaled_ffn * unit_ffn, axis=-1, keepdims=True))
    ).astype(jnp.bfloat16)
    d_attn_t = jnp.einsum("de,re->dr", w_out, d_resid, preferred_element_type=jnp.float32).astype(
        jnp.bfloat16
    )
    d_heads = jnp.broadcast_to(
        d_attn_t.reshape(HEADS, 1, head_dim, rows), (HEADS, slices, head_dim, rows)
    ).reshape(seq_size, head_dim, rows)
    grads = lax.dynamic_slice_in_dim(all_to_all(d_heads), my_slice * tiles_here, tiles_here, 0)

    share = width // seq_size
    grad_out_local = jnp.einsum("dr,re->de", attn_out_t, d_resid, preferred_element_type=jnp.float32)
    grad_in_local = jnp.einsum("rd,rf->df", normed_ffn, d_both, preferred_element_type=jnp.float32)
    grad_down_local = jnp.einsum("rf,rd->fd", hidden, grad_out, preferred_element_type=jnp.float32)
    down_blocks = grad_down_local.astype(jnp.bfloat16).reshape(seq_size, -1, share, width)
    bits = seq_size.bit_length() - 1
    outer = list(range(2, bits))
    one, one_left = as_bits(grad_in_local.astype(jnp.bfloat16).reshape(seq_size, share, -1))
    two, two_left = as_bits(
        jnp.concatenate(
            [grad_out_local.astype(jnp.bfloat16).reshape(seq_size, share, -1)]
            + [down_blocks[:, i] for i in range(down_blocks.shape[1])],
            axis=2,
        )
    )
    one, one_left = halve(one, one_left, 0)
    two, two_left = halve(two, two_left, 0)
    grads, one, two = lax.optimization_barrier((grads, one, two))
    one, one_left = halve(one, one_left, 1)
    two, two_left = halve(two, two_left, outer[0])

    dq, dkv, dvirt = attention_backward(lists, qkv_all, virt, grads, head_dim)
    dq, one, two = lax.optimization_barrier((dq, one, two))
    for bit in outer:
        one, one_left = halve(one, one_left, bit)
    for bit in outer[1:] + [1]:
        two, two_left = halve(two, two_left, bit)
    virt_rows = 2 * head_dim * parts // rows
    back_send = jnp.concatenate(
        [
            spread(dq),
            dkv,
            jnp.broadcast_to(
                dvirt.astype(jnp.bfloat16).reshape(virt_rows, rows), (seq_size, virt_rows, rows)
            ),
        ],
        axis=1,
    )
    back = all_to_all(back_send)
    dq_t = pick_slice(back[:, :head_dim])
    rest = back[:, head_dim:]
    if slices > 1:
        rest = jnp.sum(
            rest.reshape(HEADS, slices, -1, rows).astype(jnp.float32), axis=1
        ).astype(jnp.bfloat16)
    d_qkv_t = jnp.concatenate(
        [dq_t, rest[:, :head_dim], rest[:, head_dim : 2 * head_dim]], axis=0
    ).reshape(3 * width, rows)
    d_virt = (
        rest[:, 2 * head_dim :]
        .reshape(HEADS, 2, head_dim, parts)
        .transpose(1, 0, 2, 3)
        .reshape(2 * width, parts)
    )
    d_virtual = jnp.einsum(
        "sp,ds->pd", d_virt, query_key_value_weight[:, width:], preferred_element_type=jnp.float32
    )
    inner_vn = jnp.mean(d_virtual * unit_vn, axis=-1, keepdims=True)
    per_part = inv_vn * (d_virtual - unit_vn * inner_vn) / counts
    d_normed = jnp.einsum(
        "cr,dc->rd", d_qkv_t, query_key_value_weight, preferred_element_type=jnp.float32
    )
    d_normed = d_normed + jnp.dot(member.astype(jnp.float32), per_part, precision=HIGH_PRECISION)
    scaled_attn = d_normed * gain_attn
    d_features = (
        d_resid.astype(jnp.float32)
        + inv_attn
        * (scaled_attn - unit_attn * jnp.mean(scaled_attn * unit_attn, axis=-1, keepdims=True))
    ).astype(jnp.bfloat16)
    grad_qkv_local = jnp.einsum("rd,cr->dc", normed, d_qkv_t, preferred_element_type=jnp.float32)
    gain_local = jnp.concatenate(
        [jnp.sum(d_normed * unit_attn, axis=0), jnp.sum(d_normed_ffn * unit_ffn, axis=0)]
    )
    gain_share = 2 * width // seq_size
    gain_block = jnp.pad(
        gain_local.astype(jnp.bfloat16).reshape(seq_size, 1, gain_share),
        ((0, 0), (0, share - 1), (0, 128 - gain_share)),
    )
    late = jnp.concatenate(
        [grad_qkv_local.astype(jnp.bfloat16).reshape(seq_size, share, -1), gain_block], axis=2
    )
    late_sum = reduce_in_order(late, [0, 1] + outer)
    grad_w_in = one
    grad_w_out = two[:, :width]
    grad_w_down = jnp.concatenate(
        [two[:, c : c + width] for c in range(width, two.shape[1], width)], axis=0
    )
    my_virtual = lax.dynamic_slice_in_dim(virtual, me * share, share, 1)
    virtual_grad = jnp.einsum("pd,sp->ds", my_virtual, d_virt, preferred_element_type=jnp.float32)
    grad_qkv = jnp.concatenate(
        [late_sum[:, :width], late_sum[:, width : 3 * width] + virtual_grad], axis=1
    )
    grad_gains = late_sum[0, 3 * width : 3 * width + gain_share]
    return (layer_out, d_features, grad_qkv, grad_w_out, grad_w_in, grad_w_down, grad_gains)


def solution(mesh):
    node = P(("groups", "seq"), None)
    flat = P(("groups", "seq"))
    return jax.shard_map(
        on_device,
        mesh=mesh,
        in_specs=(node, P(), P(), P(), P(), P(), P(), node, flat, flat, node),
        out_specs=(node, node, node, node, node, node, flat),
        check_vma=False,
    )
```

```python
import functools
import math

import jax
import jax.numpy as jnp
from jax import lax
from jax.experimental import pallas as pl
from jax.experimental.pallas import tpu as pltpu
from jax.sharding import PartitionSpec as P

HEADS = 16
KT = 4
VN_DEV = 2
CAP = 30.0
EPS = 1e-06
HIGH_PRECISION = lax.Precision.HIGHEST
VMEM_BYTES = 48 * 1024 * 1024


def rms_parts(values):
    inverse = lax.rsqrt(jnp.mean(values * values, axis=-1, keepdims=True) + EPS)
    return (inverse, values * inverse)


def dot_tn(a, b):
    return lax.dot_general(a, b, (((0,), (0,)), ((), ())), preferred_element_type=jnp.float32)


def dot_nt(a, b):
    return lax.dot_general(a, b, (((1,), (1,)), ((), ())), preferred_element_type=jnp.float32)


def dot_nn(a, b):
    return jnp.dot(a, b, preferred_element_type=jnp.float32)


def tile_weights(lists_ref, qkv_ref, virt_ref, t, head_dim):
    count = lists_ref[t, KT]
    query = qkv_ref[lists_ref[t, 0], 0:head_dim, :]
    scale = 1.0 / (math.sqrt(head_dim) * CAP)
    tanhs, weights = [], []
    for j in range(KT):
        keys = qkv_ref[lists_ref[t, j], head_dim : 2 * head_dim, :]
        th = jnp.tanh(dot_tn(keys, query) * scale)
        w = jnp.exp(CAP * th)
        if j:
            w = w * jnp.where(j < count, 1.0, 0.0)
        tanhs.append(th)
        weights.append(w)
    th = jnp.tanh(dot_tn(virt_ref[0], query) * scale)
    tanhs.append(th)
    weights.append(jnp.exp(CAP * th))
    total = jnp.sum(weights[0], axis=0, keepdims=True)
    for w in weights[1:]:
        total = total + jnp.sum(w, axis=0, keepdims=True)
    inverse = 1.0 / total
    return query, tanhs, [w * inverse for w in weights]


def forward_kernel(
    head_dim, slices, size, lists_ref, qkv_ref, virt_ref, heads_ref, out_ref, send, recv
):
    me = lax.axis_index("seq")
    tiles_here = size // slices
    my_head = me // slices
    my_slice = me % slices
    from_slice = me // tiles_here

    def copy(t, head, to):
        return pltpu.make_async_remote_copy(
            src_ref=out_ref.at[t],
            dst_ref=heads_ref.at[head],
            send_sem=send.at[t],
            recv_sem=recv.at[head],
            device_id={"seq": to},
            device_id_type=pl.DeviceIdType.MESH,
        )

    def tile_rows(t):
        _, _, probs = tile_weights(lists_ref, qkv_ref, virt_ref, t, head_dim)
        out = dot_nn(virt_ref[1], probs[KT].astype(jnp.bfloat16))
        for j in range(KT):
            values = qkv_ref[lists_ref[t, j], 2 * head_dim : 3 * head_dim, :]
            out = out + dot_nn(values, probs[j].astype(jnp.bfloat16))
        return out.astype(jnp.bfloat16)

    barrier = pltpu.get_barrier_semaphore()

    def greet(k, carry):
        pl.semaphore_signal(
            barrier,
            inc=1,
            device_id={"seq": lax.rem(me + k, size)},
            device_id_type=pl.DeviceIdType.MESH,
        )
        return carry

    lax.fori_loop(1, size, greet, 0)
    pl.semaphore_wait(barrier, size - 1)

    def body(k, carry):
        pair = [lax.rem(me + 2 * k + 1 + u, tiles_here) for u in range(2)]
        rows = [tile_rows(t) for t in pair]
        for t, values in zip(pair, rows):
            out_ref[t] = values
        for t in pair:
            to = my_slice * tiles_here + t

            @pl.when(to != me)
            def _():
                copy(t, my_head, to).start()

            @pl.when(to == me)
            def _():
                heads_ref[my_head] = out_ref[t]

        return carry

    lax.fori_loop(0, tiles_here // 2, body, 0)

    def arrive(head, carry):
        @pl.when(head * slices + from_slice != me)
        def _():
            copy(0, head, me).wait_recv()

        return carry

    lax.fori_loop(0, HEADS, arrive, 0)

    def leave(t, carry):
        @pl.when(my_slice * tiles_here + t != me)
        def _():
            copy(t, my_head, me).wait_send()

        return carry

    lax.fori_loop(0, tiles_here, leave, 0)


def backward_kernel(
    head_dim, lists_ref, qkv_ref, virt_ref, grad_ref, dq_ref, dkv_ref, dvirt_ref, acc_ref
):
    scale = 1.0 / math.sqrt(head_dim)
    acc_ref[...] = jnp.zeros_like(acc_ref)
    dvirt_ref[...] = jnp.zeros_like(dvirt_ref)

    def body(t, carry):
        query, tanhs, probs = tile_weights(lists_ref, qkv_ref, virt_ref, t, head_dim)
        grad = grad_ref[t]
        dps = []
        for j in range(KT):
            values = qkv_ref[lists_ref[t, j], 2 * head_dim : 3 * head_dim, :]
            dps.append(dot_tn(values, grad))
        dps.append(dot_tn(virt_ref[1], grad))
        inner = jnp.sum(probs[0] * dps[0], axis=0, keepdims=True)
        for j in range(1, KT + 1):
            inner = inner + jnp.sum(probs[j] * dps[j], axis=0, keepdims=True)
        ds = [
            (p * (dp - inner) * (1.0 - th * th) * scale).astype(jnp.bfloat16)
            for p, dp, th in zip(probs, dps, tanhs)
        ]
        pb = [p.astype(jnp.bfloat16) for p in probs]
        dq = dot_nn(virt_ref[0], ds[KT])
        for j in range(KT):
            dq = dq + dot_nn(qkv_ref[lists_ref[t, j], head_dim : 2 * head_dim, :], ds[j])
        dq_ref[t] = dq.astype(jnp.bfloat16)
        for j in range(KT):
            target = lists_ref[t, j]
            acc_ref[target, 0:head_dim, :] += dot_nt(query, ds[j])
            acc_ref[target, head_dim : 2 * head_dim, :] += dot_nt(grad, pb[j])
        dvirt_ref[0:head_dim, :] += dot_nt(query, ds[KT])
        dvirt_ref[head_dim : 2 * head_dim, :] += dot_nt(grad, pb[KT])
        return carry

    lax.fori_loop(0, grad_ref.shape[0], body, 0)
    dkv_ref[...] = acc_ref[...].astype(jnp.bfloat16)


def attention_forward(lists, qkv_all, virt, head_dim, slices):
    tiles_here = lists.shape[0]
    size, _, rows = qkv_all.shape
    pairs = tiles_here * rows * (KT * rows + virt.shape[2])
    vmem = pl.BlockSpec(memory_space=pltpu.VMEM)
    return pl.pallas_call(
        functools.partial(forward_kernel, head_dim, slices, size),
        out_shape=jax.ShapeDtypeStruct((HEADS, head_dim, rows), jnp.bfloat16),
        in_specs=[pl.BlockSpec(memory_space=pltpu.SMEM), vmem, vmem],
        out_specs=vmem,
        scratch_shapes=[
            pltpu.VMEM((tiles_here, head_dim, rows), jnp.bfloat16),
            pltpu.SemaphoreType.DMA((tiles_here,)),
            pltpu.SemaphoreType.DMA((HEADS,)),
        ],
        compiler_params=pltpu.CompilerParams(
            vmem_limit_bytes=VMEM_BYTES, collective_id=1, has_side_effects=True
        ),
        cost_estimate=pl.CostEstimate(
            flops=4 * pairs * head_dim, bytes_accessed=2 * qkv_all.size, transcendentals=2 * pairs
        ),
    )(lists, qkv_all, virt)


def attention_backward(lists, qkv_all, virt, grads, head_dim):
    tiles_here, _, rows = grads.shape
    tiles = qkv_all.shape[0]
    parts = virt.shape[2]
    pairs = tiles_here * rows * (KT * rows + parts)
    vmem = pl.BlockSpec(memory_space=pltpu.VMEM)
    return pl.pallas_call(
        functools.partial(backward_kernel, head_dim),
        out_shape=(
            jax.ShapeDtypeStruct((tiles_here, head_dim, rows), jnp.bfloat16),
            jax.ShapeDtypeStruct((tiles, 2 * head_dim, rows), jnp.bfloat16),
            jax.ShapeDtypeStruct((2 * head_dim, parts), jnp.float32),
        ),
        in_specs=[pl.BlockSpec(memory_space=pltpu.SMEM), vmem, vmem, vmem],
        out_specs=(vmem, vmem, vmem),
        scratch_shapes=[pltpu.VMEM((tiles, 2 * head_dim, rows), jnp.float32)],
        compiler_params=pltpu.CompilerParams(vmem_limit_bytes=VMEM_BYTES),
        cost_estimate=pl.CostEstimate(
            flops=10 * pairs * head_dim, bytes_accessed=6 * qkv_all.size, transcendentals=2 * pairs
        ),
    )(lists, qkv_all, virt, grads)


def all_to_all(blocks):
    return lax.all_to_all(blocks, "seq", split_axis=0, concat_axis=0, tiled=True)


def as_bits(blocks):
    bits = blocks.shape[0].bit_length() - 1
    return blocks.reshape((2,) * bits + blocks.shape[1:]), list(range(bits - 1, -1, -1))


def halve(held, left, bit, after=None):
    size = lax.axis_size("seq")
    mine = (lax.axis_index("seq") // (1 << bit)) % 2
    axis = left.index(bit)
    keep = lax.dynamic_index_in_dim(held, mine, axis, keepdims=False)
    send = lax.dynamic_index_in_dim(held, 1 - mine, axis, keepdims=False)
    got = lax.ppermute(send, "seq", [(i, i ^ (1 << bit)) for i in range(size)])
    if after is not None:
        got, _ = lax.optimization_barrier((got, after))
    total = keep.astype(jnp.float32) + got.astype(jnp.float32)
    rest = [b for b in left if b != bit]
    return (total if not rest else total.astype(jnp.bfloat16)), rest


def exchange_kernel(
    slices, sums_ref, list_ref, qkv_ref, qkv_all_ref, second_ref, first_ref, own_ref, send, recv
):
    size = qkv_all_ref.shape[0]
    me = lax.axis_index("seq")

    def peer(k):
        return lax.rem(me + k, size)

    def each(step):
        def body(k, carry):
            step(k, peer(k))
            return carry

        lax.fori_loop(1, size, body, 0)

    def remote(src, dst, which, k, to):
        return pltpu.make_async_remote_copy(
            src_ref=src,
            dst_ref=dst,
            send_sem=send.at[which, k],
            recv_sem=recv.at[which, k],
            device_id={"seq": to},
            device_id_type=pl.DeviceIdType.MESH,
        )

    def first_copy(k, to):
        return remote(sums_ref.at[to], first_ref.at[me], 0, k, to)

    def second_copy(k, to):
        return remote(own_ref, second_ref.at[me], 1, k, to)

    def head_copy(k, to):
        return remote(qkv_ref.at[to // slices], qkv_all_ref.at[me], 2, k, to)

    barrier = pltpu.get_barrier_semaphore()
    each(
        lambda k, to: pl.semaphore_signal(
            barrier, inc=1, device_id={"seq": to}, device_id_type=pl.DeviceIdType.MESH
        )
    )
    first_ref[me] = sums_ref[me]
    qkv_all_ref[me] = qkv_ref[me // slices]
    pl.semaphore_wait(barrier, size - 1)
    each(lambda k, to: first_copy(k, to).start())
    each(lambda k, to: head_copy(k, to).start())
    each(lambda k, to: first_copy(k, to).wait_recv())
    own_ref[...] = (
        list_ref[...] + jnp.sum(first_ref[...].astype(jnp.float32), axis=0)
    ).astype(own_ref.dtype)
    each(lambda k, to: second_copy(k, to).start())
    second_ref[me] = own_ref[...]
    each(lambda k, to: second_copy(k, to).wait_recv())
    each(lambda k, to: head_copy(k, to).wait_recv())
    each(lambda k, to: first_copy(k, to).wait_send())
    each(lambda k, to: second_copy(k, to).wait_send())
    each(lambda k, to: head_copy(k, to).wait_send())


def exchange(sums, list_rows, qkv_heads, slices):
    size = sums.shape[0]
    vmem = pl.BlockSpec(memory_space=pltpu.VMEM)
    return pl.pallas_call(
        functools.partial(exchange_kernel, slices),
        out_shape=(
            jax.ShapeDtypeStruct((size,) + qkv_heads.shape[1:], qkv_heads.dtype),
            jax.ShapeDtypeStruct(sums.shape, sums.dtype),
        ),
        in_specs=[vmem, vmem, vmem],
        out_specs=(vmem, vmem),
        scratch_shapes=[
            pltpu.VMEM(sums.shape, sums.dtype),
            pltpu.VMEM(sums.shape[1:], sums.dtype),
            pltpu.SemaphoreType.DMA((3, size)),
            pltpu.SemaphoreType.DMA((3, size)),
        ],
        compiler_params=pltpu.CompilerParams(
            vmem_limit_bytes=VMEM_BYTES, collective_id=0, has_side_effects=True
        ),
        cost_estimate=pl.CostEstimate(
            flops=sums.size, bytes_accessed=4 * size * qkv_heads[0].size, transcendentals=0
        ),
    )(sums, list_rows, qkv_heads)


def on_device(
    features,
    gain_attn,
    gain_ffn,
    query_key_value_weight,
    w_out,
    w_in,
    w_down,
    tile_lists,
    tile_count,
    partition,
    grad_out,
):
    rows, width = features.shape
    head_dim = width // HEADS
    hidden_units = w_down.shape[0]
    seq_size = lax.axis_size("seq")
    me = lax.axis_index("seq")
    parts = VN_DEV * seq_size
    slices = seq_size // HEADS
    my_head = me // slices
    my_slice = me % slices
    tiles_here = seq_size // slices
    slice_of_me = me // tiles_here

    x_f = features.astype(jnp.float32)
    inv_attn, unit_attn = rms_parts(x_f)
    normed = (unit_attn * gain_attn).astype(jnp.bfloat16)
    member = (partition[:, None] == jnp.arange(parts, dtype=jnp.int32)[None, :]).astype(
        jnp.bfloat16
    )
    part_sums = jnp.einsum("rp,rd->pd", member, normed, preferred_element_type=jnp.float32)
    part_counts = jnp.sum(member.astype(jnp.float32), axis=0)
    lanes = 128
    sum_rows = VN_DEV * width // lanes
    list_at = sum_rows + VN_DEV
    block_rows = -(-(list_at + 1) // 16) * 16
    sums = jnp.concatenate(
        [
            part_sums.reshape(seq_size, sum_rows, lanes),
            jnp.broadcast_to(
                part_counts.reshape(seq_size, VN_DEV, 1), (seq_size, VN_DEV, lanes)
            ),
            jnp.zeros((seq_size, block_rows - list_at, lanes), jnp.float32),
        ],
        axis=1,
    ).astype(jnp.bfloat16)
    list_rows = jnp.pad(
        jnp.concatenate([tile_lists[0], tile_count]).astype(jnp.float32)[None],
        ((list_at, block_rows - list_at - 1), (0, lanes - KT - 1)),
    )
    qkv = jnp.dot(normed, query_key_value_weight, preferred_element_type=jnp.float32)
    qkv_t = lax.optimization_barrier(qkv.astype(jnp.bfloat16)).T
    qkv_heads = jnp.transpose(qkv_t.reshape(3, HEADS, head_dim, rows), (1, 0, 2, 3)).reshape(
        HEADS, 3 * head_dim, rows
    )
    qkv_all, second = exchange(sums, list_rows, qkv_heads, slices)
    second = second.astype(jnp.float32)
    totals = second[:, :sum_rows].reshape(parts, width)
    counts = second[:, sum_rows:list_at, :1].reshape(parts, 1)
    lists_all = second[:, list_at, : KT + 1].astype(jnp.int32)
    part_mean = totals / counts
    inv_vn, unit_vn = rms_parts(part_mean)
    virtual = unit_vn.astype(jnp.bfloat16)

    lists = lax.dynamic_slice_in_dim(lists_all, my_slice * tiles_here, tiles_here, 0)
    weight_heads = query_key_value_weight.reshape(width, 3, HEADS, head_dim)
    my_columns = lax.dynamic_index_in_dim(weight_heads, my_head, 2, keepdims=False)[:, 1:]
    virt = jnp.einsum(
        "dke,pd->kep", my_columns, virtual, preferred_element_type=jnp.float32
    ).astype(jnp.bfloat16)

    def spread(local):
        if slices == 1:
            return local
        empty = jnp.zeros((seq_size,) + local.shape[1:], local.dtype)
        return lax.dynamic_update_slice_in_dim(empty, local, my_slice * tiles_here, 0)

    def pick_slice(received):
        split = received.reshape((HEADS, slices) + received.shape[1:])
        return lax.dynamic_index_in_dim(split, slice_of_me, 1, keepdims=False)

    attn_out_t = attention_forward(lists, qkv_all, virt, head_dim, slices).reshape(width, rows)

    mixed = jnp.einsum("dr,de->re", attn_out_t, w_out, preferred_element_type=jnp.float32)
    resid = (x_f + mixed).astype(jnp.bfloat16)
    res_f = resid.astype(jnp.float32)
    inv_ffn, unit_ffn = rms_parts(res_f)
    normed_ffn = (unit_ffn * gain_ffn).astype(jnp.bfloat16)
    gate_up = jnp.dot(normed_ffn, w_in, preferred_element_type=jnp.float32)
    gate_proj = gate_up[:, :hidden_units]
    up_proj = gate_up[:, hidden_units:]
    sigmoid_gate = jax.nn.sigmoid(gate_proj)
    activated = gate_proj * sigmoid_gate
    hidden = (activated * up_proj).astype(jnp.bfloat16)
    layer_out = (res_f + jnp.dot(hidden, w_down, preferred_element_type=jnp.float32)).astype(
        jnp.bfloat16
    )
    d_hidden = jnp.einsum("rd,fd->rf", grad_out, w_down, preferred_element_type=jnp.float32)
    d_gate = d_hidden * up_proj * sigmoid_gate * (1.0 + gate_proj * (1.0 - sigmoid_gate))
    d_up = d_hidden * activated
    d_both = jnp.concatenate([d_gate, d_up], axis=1).astype(jnp.bfloat16)
    d_normed_ffn = jnp.einsum("rf,df->rd", d_both, w_in, preferred_element_type=jnp.float32)
    scaled_ffn = d_normed_ffn * gain_ffn
    d_resid = (
        grad_out.astype(jnp.float32)
        + inv_ffn
        * (scaled_ffn - unit_ffn * jnp.mean(scaled_ffn * unit_ffn, axis=-1, keepdims=True))
    ).astype(jnp.bfloat16)
    d_attn_t = jnp.einsum("de,re->dr", w_out, d_resid, preferred_element_type=jnp.float32).astype(
        jnp.bfloat16
    )
    d_heads = jnp.broadcast_to(
        d_attn_t.reshape(HEADS, 1, head_dim, rows), (HEADS, slices, head_dim, rows)
    ).reshape(seq_size, head_dim, rows)
    grads = lax.dynamic_slice_in_dim(all_to_all(d_heads), my_slice * tiles_here, tiles_here, 0)

    share = width // seq_size
    grad_out_local = jnp.einsum("dr,re->de", attn_out_t, d_resid, preferred_element_type=jnp.float32)
    grad_in_local = jnp.einsum("rd,rf->df", normed_ffn, d_both, preferred_element_type=jnp.float32)
    grad_down_local = jnp.einsum("rf,rd->fd", hidden, grad_out, preferred_element_type=jnp.float32)
    down_blocks = grad_down_local.astype(jnp.bfloat16).reshape(seq_size, -1, share, width)
    bits = seq_size.bit_length() - 1
    outer = list(range(2, bits))
    one, one_left = as_bits(grad_in_local.astype(jnp.bfloat16).reshape(seq_size, share, -1))
    two, two_left = as_bits(
        jnp.concatenate(
            [grad_out_local.astype(jnp.bfloat16).reshape(seq_size, share, -1)]
            + [down_blocks[:, i] for i in range(down_blocks.shape[1])],
            axis=2,
        )
    )
    one, one_left = halve(one, one_left, 0)
    two, two_left = halve(two, two_left, 0)
    grads, one, two = lax.optimization_barrier((grads, one, two))
    one, one_left = halve(one, one_left, 1)
    two, two_left = halve(two, two_left, outer[0])
    one_order = outer
    two_order = outer[1:] + [1]

    dq, dkv, dvirt = attention_backward(lists, qkv_all, virt, grads, head_dim)
    dq, one, two = lax.optimization_barrier((dq, one, two))
    virt_rows = 2 * head_dim * parts // rows
    back_send = jnp.concatenate(
        [
            spread(dq),
            dkv,
            jnp.broadcast_to(
                dvirt.astype(jnp.bfloat16).reshape(virt_rows, rows), (seq_size, virt_rows, rows)
            ),
        ],
        axis=1,
    )
    back = all_to_all(back_send)
    dq_t = pick_slice(back[:, :head_dim])
    rest = back[:, head_dim:]
    if slices > 1:
        rest = jnp.sum(
            rest.reshape(HEADS, slices, -1, rows).astype(jnp.float32), axis=1
        ).astype(jnp.bfloat16)
    d_qkv_t = jnp.concatenate(
        [dq_t, rest[:, :head_dim], rest[:, head_dim : 2 * head_dim]], axis=0
    ).reshape(3 * width, rows)
    d_virt = (
        rest[:, 2 * head_dim :]
        .reshape(HEADS, 2, head_dim, parts)
        .transpose(1, 0, 2, 3)
        .reshape(2 * width, parts)
    )
    d_virtual = jnp.einsum(
        "sp,ds->pd", d_virt, query_key_value_weight[:, width:], preferred_element_type=jnp.float32
    )
    inner_vn = jnp.mean(d_virtual * unit_vn, axis=-1, keepdims=True)
    per_part = inv_vn * (d_virtual - unit_vn * inner_vn) / counts
    grad_qkv_local = jnp.einsum("rd,cr->dc", normed, d_qkv_t, preferred_element_type=jnp.float32)
    late = grad_qkv_local.astype(jnp.bfloat16).reshape(seq_size, share, -1)
    for step, bit in enumerate(one_order):
        one, one_left = halve(one, one_left, bit, late if step == 0 else None)
    for step, bit in enumerate(two_order):
        two, two_left = halve(two, two_left, bit, late if step == 0 else None)
    late, late_left = as_bits(late)
    late, late_left = halve(late, late_left, 0)
    middle = late.shape[-1] // 2
    late_one, late_two = late[..., :middle], late[..., middle:]
    one_left, two_left = late_left, late_left
    for one_bit, two_bit in zip([1] + outer, outer + [1]):
        late_one, one_left = halve(late_one, one_left, one_bit)
        late_two, two_left = halve(late_two, two_left, two_bit)
    late_sum = jnp.concatenate([late_one, late_two], axis=1)
    d_normed = jnp.einsum(
        "cr,dc->rd", d_qkv_t, query_key_value_weight, preferred_element_type=jnp.float32
    )
    d_normed = d_normed + jnp.dot(member.astype(jnp.float32), per_part, precision=HIGH_PRECISION)
    scaled_attn = d_normed * gain_attn
    d_features = (
        d_resid.astype(jnp.float32)
        + inv_attn
        * (scaled_attn - unit_attn * jnp.mean(scaled_attn * unit_attn, axis=-1, keepdims=True))
    ).astype(jnp.bfloat16)
    gain_local = jnp.concatenate(
        [jnp.sum(d_normed * unit_attn, axis=0), jnp.sum(d_normed_ffn * unit_ffn, axis=0)]
    )
    gain_share = 2 * width // seq_size
    grad_gains = jnp.sum(all_to_all(gain_local.reshape(seq_size, gain_share)), axis=0)
    grad_w_in = one
    grad_w_out = two[:, :width]
    grad_w_down = jnp.concatenate(
        [two[:, c : c + width] for c in range(width, two.shape[1], width)], axis=0
    )
    my_virtual = lax.dynamic_slice_in_dim(virtual, me * share, share, 1)
    virtual_grad = jnp.einsum("pd,sp->ds", my_virtual, d_virt, preferred_element_type=jnp.float32)
    grad_qkv = jnp.concatenate(
        [late_sum[:, :width], late_sum[:, width : 3 * width] + virtual_grad], axis=1
    )
    return (layer_out, d_features, grad_qkv, grad_w_out, grad_w_in, grad_w_down, grad_gains)


def solution(mesh):
    node = P(("groups", "seq"), None)
    flat = P(("groups", "seq"))
    return jax.shard_map(
        on_device,
        mesh=mesh,
        in_specs=(node, P(), P(), P(), P(), P(), P(), node, flat, flat, node),
        out_specs=(node, node, node, node, node, node, flat),
        check_vma=False,
    )
```

```python
import functools
import math

import jax
import jax.numpy as jnp
from jax import lax
from jax.experimental import pallas as pl
from jax.experimental.pallas import tpu as pltpu
from jax.sharding import PartitionSpec as P

HEADS = 16
KT = 4
VN_DEV = 2
CAP = 30.0
EPS = 1e-06
HIGH_PRECISION = lax.Precision.HIGHEST
VMEM_BYTES = 48 * 1024 * 1024


def rms_parts(values):
    inverse = lax.rsqrt(jnp.mean(values * values, axis=-1, keepdims=True) + EPS)
    return (inverse, values * inverse)


def dot_tn(a, b):
    return lax.dot_general(a, b, (((0,), (0,)), ((), ())), preferred_element_type=jnp.float32)


def dot_nt(a, b):
    return lax.dot_general(a, b, (((1,), (1,)), ((), ())), preferred_element_type=jnp.float32)


def dot_nn(a, b):
    return jnp.dot(a, b, preferred_element_type=jnp.float32)


def tile_weights(lists_ref, qkv_ref, virt_ref, t, head_dim):
    count = lists_ref[t, KT]
    query = qkv_ref[lists_ref[t, 0], 0:head_dim, :]
    scale = 1.0 / (math.sqrt(head_dim) * CAP)
    tanhs, weights = [], []
    for j in range(KT):
        keys = qkv_ref[lists_ref[t, j], head_dim : 2 * head_dim, :]
        th = jnp.tanh(dot_tn(keys, query) * scale)
        w = jnp.exp(CAP * th)
        if j:
            w = w * jnp.where(j < count, 1.0, 0.0)
        tanhs.append(th)
        weights.append(w)
    th = jnp.tanh(dot_tn(virt_ref[0], query) * scale)
    tanhs.append(th)
    weights.append(jnp.exp(CAP * th))
    total = jnp.sum(weights[0], axis=0, keepdims=True)
    for w in weights[1:]:
        total = total + jnp.sum(w, axis=0, keepdims=True)
    inverse = 1.0 / total
    return query, tanhs, [w * inverse for w in weights]


def forward_kernel(
    head_dim, slices, size, lists_ref, qkv_ref, virt_ref, heads_ref, out_ref, send, recv
):
    me = lax.axis_index("seq")
    tiles_here = size // slices
    my_head = me // slices
    my_slice = me % slices
    from_slice = me // tiles_here

    def copy(t, head, to):
        return pltpu.make_async_remote_copy(
            src_ref=out_ref.at[t],
            dst_ref=heads_ref.at[head],
            send_sem=send.at[t],
            recv_sem=recv.at[head],
            device_id={"seq": to},
            device_id_type=pl.DeviceIdType.MESH,
        )

    def tile_rows(t):
        _, _, probs = tile_weights(lists_ref, qkv_ref, virt_ref, t, head_dim)
        out = dot_nn(virt_ref[1], probs[KT].astype(jnp.bfloat16))
        for j in range(KT):
            values = qkv_ref[lists_ref[t, j], 2 * head_dim : 3 * head_dim, :]
            out = out + dot_nn(values, probs[j].astype(jnp.bfloat16))
        return out.astype(jnp.bfloat16)

    barrier = pltpu.get_barrier_semaphore()

    def greet(k, carry):
        pl.semaphore_signal(
            barrier,
            inc=1,
            device_id={"seq": lax.rem(me + k, size)},
            device_id_type=pl.DeviceIdType.MESH,
        )
        return carry

    lax.fori_loop(1, size, greet, 0)
    pl.semaphore_wait(barrier, size - 1)

    def body(k, carry):
        pair = [lax.rem(me + 2 * k + 1 + u, tiles_here) for u in range(2)]
        rows = [tile_rows(t) for t in pair]
        for t, values in zip(pair, rows):
            out_ref[t] = values
        for t in pair:
            to = my_slice * tiles_here + t

            @pl.when(to != me)
            def _():
                copy(t, my_head, to).start()

            @pl.when(to == me)
            def _():
                heads_ref[my_head] = out_ref[t]

        return carry

    lax.fori_loop(0, tiles_here // 2, body, 0)

    def arrive(head, carry):
        @pl.when(head * slices + from_slice != me)
        def _():
            copy(0, head, me).wait_recv()

        return carry

    lax.fori_loop(0, HEADS, arrive, 0)

    def leave(t, carry):
        @pl.when(my_slice * tiles_here + t != me)
        def _():
            copy(t, my_head, me).wait_send()

        return carry

    lax.fori_loop(0, tiles_here, leave, 0)


def backward_kernel(
    head_dim, lists_ref, qkv_ref, virt_ref, grad_ref, dq_ref, dkv_ref, dvirt_ref, acc_ref
):
    scale = 1.0 / math.sqrt(head_dim)
    acc_ref[...] = jnp.zeros_like(acc_ref)
    dvirt_ref[...] = jnp.zeros_like(dvirt_ref)

    def body(t, carry):
        query, tanhs, probs = tile_weights(lists_ref, qkv_ref, virt_ref, t, head_dim)
        grad = grad_ref[t]
        dps = []
        for j in range(KT):
            values = qkv_ref[lists_ref[t, j], 2 * head_dim : 3 * head_dim, :]
            dps.append(dot_tn(values, grad))
        dps.append(dot_tn(virt_ref[1], grad))
        inner = jnp.sum(probs[0] * dps[0], axis=0, keepdims=True)
        for j in range(1, KT + 1):
            inner = inner + jnp.sum(probs[j] * dps[j], axis=0, keepdims=True)
        ds = [
            (p * (dp - inner) * (1.0 - th * th) * scale).astype(jnp.bfloat16)
            for p, dp, th in zip(probs, dps, tanhs)
        ]
        pb = [p.astype(jnp.bfloat16) for p in probs]
        dq = dot_nn(virt_ref[0], ds[KT])
        for j in range(KT):
            dq = dq + dot_nn(qkv_ref[lists_ref[t, j], head_dim : 2 * head_dim, :], ds[j])
        dq_ref[t] = dq.astype(jnp.bfloat16)
        for j in range(KT):
            target = lists_ref[t, j]
            acc_ref[target, 0:head_dim, :] += dot_nt(query, ds[j])
            acc_ref[target, head_dim : 2 * head_dim, :] += dot_nt(grad, pb[j])
        dvirt_ref[0:head_dim, :] += dot_nt(query, ds[KT])
        dvirt_ref[head_dim : 2 * head_dim, :] += dot_nt(grad, pb[KT])
        return carry

    lax.fori_loop(0, grad_ref.shape[0], body, 0, unroll=2)
    dkv_ref[...] = acc_ref[...].astype(jnp.bfloat16)


def attention_forward(lists, qkv_all, virt, head_dim, slices):
    tiles_here = lists.shape[0]
    size, _, rows = qkv_all.shape
    pairs = tiles_here * rows * (KT * rows + virt.shape[2])
    vmem = pl.BlockSpec(memory_space=pltpu.VMEM)
    return pl.pallas_call(
        functools.partial(forward_kernel, head_dim, slices, size),
        out_shape=jax.ShapeDtypeStruct((HEADS, head_dim, rows), jnp.bfloat16),
        in_specs=[pl.BlockSpec(memory_space=pltpu.SMEM), vmem, vmem],
        out_specs=vmem,
        scratch_shapes=[
            pltpu.VMEM((tiles_here, head_dim, rows), jnp.bfloat16),
            pltpu.SemaphoreType.DMA((tiles_here,)),
            pltpu.SemaphoreType.DMA((HEADS,)),
        ],
        compiler_params=pltpu.CompilerParams(
            vmem_limit_bytes=VMEM_BYTES, collective_id=1, has_side_effects=True
        ),
        cost_estimate=pl.CostEstimate(
            flops=4 * pairs * head_dim, bytes_accessed=2 * qkv_all.size, transcendentals=2 * pairs
        ),
    )(lists, qkv_all, virt)


def attention_backward(lists, qkv_all, virt, grads, head_dim):
    tiles_here, _, rows = grads.shape
    tiles = qkv_all.shape[0]
    parts = virt.shape[2]
    pairs = tiles_here * rows * (KT * rows + parts)
    vmem = pl.BlockSpec(memory_space=pltpu.VMEM)
    return pl.pallas_call(
        functools.partial(backward_kernel, head_dim),
        out_shape=(
            jax.ShapeDtypeStruct((tiles_here, head_dim, rows), jnp.bfloat16),
            jax.ShapeDtypeStruct((tiles, 2 * head_dim, rows), jnp.bfloat16),
            jax.ShapeDtypeStruct((2 * head_dim, parts), jnp.float32),
        ),
        in_specs=[pl.BlockSpec(memory_space=pltpu.SMEM), vmem, vmem, vmem],
        out_specs=(vmem, vmem, vmem),
        scratch_shapes=[pltpu.VMEM((tiles, 2 * head_dim, rows), jnp.float32)],
        compiler_params=pltpu.CompilerParams(vmem_limit_bytes=VMEM_BYTES),
        cost_estimate=pl.CostEstimate(
            flops=10 * pairs * head_dim, bytes_accessed=6 * qkv_all.size, transcendentals=2 * pairs
        ),
    )(lists, qkv_all, virt, grads)


def all_to_all(blocks):
    return lax.all_to_all(blocks, "seq", split_axis=0, concat_axis=0, tiled=True)


def as_bits(blocks):
    bits = blocks.shape[0].bit_length() - 1
    return blocks.reshape((2,) * bits + blocks.shape[1:]), list(range(bits - 1, -1, -1))


def halve(held, left, bit, after=None):
    size = lax.axis_size("seq")
    mine = (lax.axis_index("seq") // (1 << bit)) % 2
    axis = left.index(bit)
    keep = lax.dynamic_index_in_dim(held, mine, axis, keepdims=False)
    send = lax.dynamic_index_in_dim(held, 1 - mine, axis, keepdims=False)
    got = lax.ppermute(send, "seq", [(i, i ^ (1 << bit)) for i in range(size)])
    if after is not None:
        got, _ = lax.optimization_barrier((got, after))
    total = keep.astype(jnp.float32) + got.astype(jnp.float32)
    rest = [b for b in left if b != bit]
    return (total if not rest else total.astype(jnp.bfloat16)), rest


def exchange_kernel(
    slices, sums_ref, list_ref, qkv_ref, qkv_all_ref, second_ref, first_ref, own_ref, send, recv
):
    size = qkv_all_ref.shape[0]
    me = lax.axis_index("seq")

    def peer(k):
        return lax.rem(me + k, size)

    def each(step):
        def body(k, carry):
            step(k, peer(k))
            return carry

        lax.fori_loop(1, size, body, 0)

    def remote(src, dst, which, k, to):
        return pltpu.make_async_remote_copy(
            src_ref=src,
            dst_ref=dst,
            send_sem=send.at[which, k],
            recv_sem=recv.at[which, k],
            device_id={"seq": to},
            device_id_type=pl.DeviceIdType.MESH,
        )

    def first_copy(k, to):
        return remote(sums_ref.at[to], first_ref.at[me], 0, k, to)

    def second_copy(k, to):
        return remote(own_ref, second_ref.at[me], 1, k, to)

    def head_copy(k, to):
        return remote(qkv_ref.at[to // slices], qkv_all_ref.at[me], 2, k, to)

    barrier = pltpu.get_barrier_semaphore()
    each(
        lambda k, to: pl.semaphore_signal(
            barrier, inc=1, device_id={"seq": to}, device_id_type=pl.DeviceIdType.MESH
        )
    )
    first_ref[me] = sums_ref[me]
    qkv_all_ref[me] = qkv_ref[me // slices]
    pl.semaphore_wait(barrier, size - 1)
    each(lambda k, to: first_copy(k, to).start())
    each(lambda k, to: head_copy(k, to).start())
    each(lambda k, to: first_copy(k, to).wait_recv())
    own_ref[...] = (
        list_ref[...] + jnp.sum(first_ref[...].astype(jnp.float32), axis=0)
    ).astype(own_ref.dtype)
    each(lambda k, to: second_copy(k, to).start())
    second_ref[me] = own_ref[...]
    each(lambda k, to: second_copy(k, to).wait_recv())
    each(lambda k, to: head_copy(k, to).wait_recv())
    each(lambda k, to: first_copy(k, to).wait_send())
    each(lambda k, to: second_copy(k, to).wait_send())
    each(lambda k, to: head_copy(k, to).wait_send())


def exchange(sums, list_rows, qkv_heads, slices):
    size = sums.shape[0]
    vmem = pl.BlockSpec(memory_space=pltpu.VMEM)
    return pl.pallas_call(
        functools.partial(exchange_kernel, slices),
        out_shape=(
            jax.ShapeDtypeStruct((size,) + qkv_heads.shape[1:], qkv_heads.dtype),
            jax.ShapeDtypeStruct(sums.shape, sums.dtype),
        ),
        in_specs=[vmem, vmem, vmem],
        out_specs=(vmem, vmem),
        scratch_shapes=[
            pltpu.VMEM(sums.shape, sums.dtype),
            pltpu.VMEM(sums.shape[1:], sums.dtype),
            pltpu.SemaphoreType.DMA((3, size)),
            pltpu.SemaphoreType.DMA((3, size)),
        ],
        compiler_params=pltpu.CompilerParams(
            vmem_limit_bytes=VMEM_BYTES, collective_id=0, has_side_effects=True
        ),
        cost_estimate=pl.CostEstimate(
            flops=sums.size, bytes_accessed=4 * size * qkv_heads[0].size, transcendentals=0
        ),
    )(sums, list_rows, qkv_heads)


def fold_kernel(orders, *refs):
    me = lax.axis_index("seq")
    steps = len(orders[0])
    inputs, outputs, scratch = refs[:2], refs[2:4], refs[4:-2]
    send, recv = refs[-2:]
    landing = (scratch[:steps], scratch[steps : 2 * steps])
    rest = scratch[2 * steps :]
    held = (rest[: steps - 1], rest[steps - 1 :])

    def partner(bit):
        return me + (1 << bit) * (1 - 2 * ((me // (1 << bit)) % 2))

    def half(stream, step, theirs):
        bit = orders[stream][step]
        left = sorted(set(range(steps)) - set(orders[stream][:step]), reverse=True)
        mine = (me // (1 << bit)) % 2
        index = (slice(None),) * left.index(bit) + (1 - mine if theirs else mine,)
        return (inputs[stream] if step == 0 else held[stream][step - 1]), index

    def copy(stream, step):
        source, index = half(stream, step, True)
        return pltpu.make_async_remote_copy(
            src_ref=source.at[index],
            dst_ref=landing[stream][step],
            send_sem=send.at[stream, step],
            recv_sem=recv.at[stream, step],
            device_id={"seq": partner(orders[stream][step])},
            device_id_type=pl.DeviceIdType.MESH,
        )

    barrier = pltpu.get_barrier_semaphore()
    for bit in range(steps):
        pl.semaphore_signal(
            barrier,
            inc=1,
            device_id={"seq": partner(bit)},
            device_id_type=pl.DeviceIdType.MESH,
        )
    pl.semaphore_wait(barrier, steps)
    for stream in range(2):
        copy(stream, 0).start()
    for step in range(steps):
        for stream in range(2):
            copy(stream, step).wait_recv()
            source, index = half(stream, step, False)
            total = source[index].astype(jnp.float32) + landing[stream][step][...].astype(
                jnp.float32
            )
            if step == steps - 1:
                outputs[stream][...] = total
            else:
                held[stream][step][...] = total.astype(jnp.bfloat16)
                copy(stream, step + 1).start()
    for step in range(steps):
        for stream in range(2):
            copy(stream, step).wait_send()


def fold(one, two):
    size = one.shape[0]
    steps = size.bit_length() - 1
    orders = ([0, 1] + list(range(2, steps)), [0] + list(range(2, steps)) + [1])
    vmem = pl.BlockSpec(memory_space=pltpu.VMEM)
    blocks = [as_bits(one)[0], as_bits(two)[0]]
    tails = [one.shape[1:], two.shape[1:]]
    landing = [
        pltpu.VMEM((2,) * (steps - 1 - step) + tail, jnp.bfloat16)
        for tail in tails
        for step in range(steps)
    ]
    held = [
        pltpu.VMEM((2,) * (steps - 1 - step) + tail, jnp.bfloat16)
        for tail in tails
        for step in range(steps - 1)
    ]
    return pl.pallas_call(
        functools.partial(fold_kernel, orders),
        out_shape=tuple(jax.ShapeDtypeStruct(tail, jnp.float32) for tail in tails),
        in_specs=[vmem, vmem],
        out_specs=(vmem, vmem),
        scratch_shapes=landing
        + held
        + [pltpu.SemaphoreType.DMA((2, steps)), pltpu.SemaphoreType.DMA((2, steps))],
        compiler_params=pltpu.CompilerParams(
            vmem_limit_bytes=VMEM_BYTES, collective_id=2, has_side_effects=True
        ),
        cost_estimate=pl.CostEstimate(
            flops=one.size, bytes_accessed=8 * (one.size + two.size), transcendentals=0
        ),
    )(*blocks)


def on_device(
    features,
    gain_attn,
    gain_ffn,
    query_key_value_weight,
    w_out,
    w_in,
    w_down,
    tile_lists,
    tile_count,
    partition,
    grad_out,
):
    rows, width = features.shape
    head_dim = width // HEADS
    hidden_units = w_down.shape[0]
    seq_size = lax.axis_size("seq")
    me = lax.axis_index("seq")
    parts = VN_DEV * seq_size
    slices = seq_size // HEADS
    my_head = me // slices
    my_slice = me % slices
    tiles_here = seq_size // slices
    slice_of_me = me // tiles_here

    x_f = features.astype(jnp.float32)
    inv_attn, unit_attn = rms_parts(x_f)
    normed = (unit_attn * gain_attn).astype(jnp.bfloat16)
    member = (partition[:, None] == jnp.arange(parts, dtype=jnp.int32)[None, :]).astype(
        jnp.bfloat16
    )
    part_sums = jnp.einsum("rp,rd->pd", member, normed, preferred_element_type=jnp.float32)
    part_counts = jnp.sum(member.astype(jnp.float32), axis=0)
    lanes = 128
    sum_rows = VN_DEV * width // lanes
    list_at = sum_rows + VN_DEV
    block_rows = -(-(list_at + 1) // 16) * 16
    sums = jnp.concatenate(
        [
            part_sums.reshape(seq_size, sum_rows, lanes),
            jnp.broadcast_to(
                part_counts.reshape(seq_size, VN_DEV, 1), (seq_size, VN_DEV, lanes)
            ),
            jnp.zeros((seq_size, block_rows - list_at, lanes), jnp.float32),
        ],
        axis=1,
    ).astype(jnp.bfloat16)
    list_rows = jnp.pad(
        jnp.concatenate([tile_lists[0], tile_count]).astype(jnp.float32)[None],
        ((list_at, block_rows - list_at - 1), (0, lanes - KT - 1)),
    )
    qkv = jnp.dot(normed, query_key_value_weight, preferred_element_type=jnp.float32)
    qkv_t = lax.optimization_barrier(qkv.astype(jnp.bfloat16)).T
    qkv_heads = jnp.transpose(qkv_t.reshape(3, HEADS, head_dim, rows), (1, 0, 2, 3)).reshape(
        HEADS, 3 * head_dim, rows
    )
    qkv_all, second = exchange(sums, list_rows, qkv_heads, slices)
    second = second.astype(jnp.float32)
    totals = second[:, :sum_rows].reshape(parts, width)
    counts = second[:, sum_rows:list_at, :1].reshape(parts, 1)
    lists_all = second[:, list_at, : KT + 1].astype(jnp.int32)
    part_mean = totals / counts
    inv_vn, unit_vn = rms_parts(part_mean)
    virtual = unit_vn.astype(jnp.bfloat16)

    lists = lax.dynamic_slice_in_dim(lists_all, my_slice * tiles_here, tiles_here, 0)
    weight_heads = query_key_value_weight.reshape(width, 3, HEADS, head_dim)
    my_columns = lax.dynamic_index_in_dim(weight_heads, my_head, 2, keepdims=False)[:, 1:]
    virt = jnp.einsum(
        "dke,pd->kep", my_columns, virtual, preferred_element_type=jnp.float32
    ).astype(jnp.bfloat16)

    def spread(local):
        if slices == 1:
            return local
        empty = jnp.zeros((seq_size,) + local.shape[1:], local.dtype)
        return lax.dynamic_update_slice_in_dim(empty, local, my_slice * tiles_here, 0)

    def pick_slice(received):
        split = received.reshape((HEADS, slices) + received.shape[1:])
        return lax.dynamic_index_in_dim(split, slice_of_me, 1, keepdims=False)

    attn_out_t = attention_forward(lists, qkv_all, virt, head_dim, slices).reshape(width, rows)

    mixed = jnp.einsum("dr,de->re", attn_out_t, w_out, preferred_element_type=jnp.float32)
    resid = (x_f + mixed).astype(jnp.bfloat16)
    res_f = resid.astype(jnp.float32)
    inv_ffn, unit_ffn = rms_parts(res_f)
    normed_ffn = (unit_ffn * gain_ffn).astype(jnp.bfloat16)
    gate_up = jnp.dot(normed_ffn, w_in, preferred_element_type=jnp.float32)
    gate_proj = gate_up[:, :hidden_units]
    up_proj = gate_up[:, hidden_units:]
    sigmoid_gate = jax.nn.sigmoid(gate_proj)
    activated = gate_proj * sigmoid_gate
    hidden = (activated * up_proj).astype(jnp.bfloat16)
    layer_out = (res_f + jnp.dot(hidden, w_down, preferred_element_type=jnp.float32)).astype(
        jnp.bfloat16
    )
    d_hidden = jnp.einsum("rd,fd->rf", grad_out, w_down, preferred_element_type=jnp.float32)
    d_gate = d_hidden * up_proj * sigmoid_gate * (1.0 + gate_proj * (1.0 - sigmoid_gate))
    d_up = d_hidden * activated
    d_both = jnp.concatenate([d_gate, d_up], axis=1).astype(jnp.bfloat16)
    d_normed_ffn = jnp.einsum("rf,df->rd", d_both, w_in, preferred_element_type=jnp.float32)
    scaled_ffn = d_normed_ffn * gain_ffn
    d_resid = (
        grad_out.astype(jnp.float32)
        + inv_ffn
        * (scaled_ffn - unit_ffn * jnp.mean(scaled_ffn * unit_ffn, axis=-1, keepdims=True))
    ).astype(jnp.bfloat16)
    d_attn_t = jnp.einsum("de,re->dr", w_out, d_resid, preferred_element_type=jnp.float32).astype(
        jnp.bfloat16
    )
    d_heads = jnp.broadcast_to(
        d_attn_t.reshape(HEADS, 1, head_dim, rows), (HEADS, slices, head_dim, rows)
    ).reshape(seq_size, head_dim, rows)
    grads = lax.dynamic_slice_in_dim(all_to_all(d_heads), my_slice * tiles_here, tiles_here, 0)

    share = width // seq_size
    grad_out_local = jnp.einsum("dr,re->de", attn_out_t, d_resid, preferred_element_type=jnp.float32)
    grad_in_local = jnp.einsum("rd,rf->df", normed_ffn, d_both, preferred_element_type=jnp.float32)
    grad_down_local = jnp.einsum("rf,rd->fd", hidden, grad_out, preferred_element_type=jnp.float32)
    down_blocks = grad_down_local.astype(jnp.bfloat16).reshape(seq_size, -1, share, width)
    bits = seq_size.bit_length() - 1
    outer = list(range(2, bits))
    one, one_left = as_bits(grad_in_local.astype(jnp.bfloat16).reshape(seq_size, share, -1))
    two, two_left = as_bits(
        jnp.concatenate(
            [grad_out_local.astype(jnp.bfloat16).reshape(seq_size, share, -1)]
            + [down_blocks[:, i] for i in range(down_blocks.shape[1])],
            axis=2,
        )
    )
    one, one_left = halve(one, one_left, 0)
    two, two_left = halve(two, two_left, 0)
    grads, one, two = lax.optimization_barrier((grads, one, two))
    one, one_left = halve(one, one_left, 1)
    two, two_left = halve(two, two_left, outer[0])
    one_order = outer
    two_order = outer[1:] + [1]

    dq, dkv, dvirt = attention_backward(lists, qkv_all, virt, grads, head_dim)
    dq, one, two = lax.optimization_barrier((dq, one, two))
    virt_rows = 2 * head_dim * parts // rows
    back_send = jnp.concatenate(
        [
            spread(dq),
            dkv,
            jnp.broadcast_to(
                dvirt.astype(jnp.bfloat16).reshape(virt_rows, rows), (seq_size, virt_rows, rows)
            ),
        ],
        axis=1,
    )
    back = all_to_all(back_send)
    dq_t = pick_slice(back[:, :head_dim])
    rest = back[:, head_dim:]
    if slices > 1:
        rest = jnp.sum(
            rest.reshape(HEADS, slices, -1, rows).astype(jnp.float32), axis=1
        ).astype(jnp.bfloat16)
    d_qkv_t = jnp.concatenate(
        [dq_t, rest[:, :head_dim], rest[:, head_dim : 2 * head_dim]], axis=0
    ).reshape(3 * width, rows)
    d_virt = (
        rest[:, 2 * head_dim :]
        .reshape(HEADS, 2, head_dim, parts)
        .transpose(1, 0, 2, 3)
        .reshape(2 * width, parts)
    )
    d_virtual = jnp.einsum(
        "sp,ds->pd", d_virt, query_key_value_weight[:, width:], preferred_element_type=jnp.float32
    )
    inner_vn = jnp.mean(d_virtual * unit_vn, axis=-1, keepdims=True)
    per_part = inv_vn * (d_virtual - unit_vn * inner_vn) / counts
    grad_qkv_local = jnp.einsum("rd,cr->dc", normed, d_qkv_t, preferred_element_type=jnp.float32)
    late = grad_qkv_local.astype(jnp.bfloat16).reshape(seq_size, share, -1)
    for step, bit in enumerate(one_order):
        one, one_left = halve(one, one_left, bit, late if step == 0 else None)
    for step, bit in enumerate(two_order):
        two, two_left = halve(two, two_left, bit, late if step == 0 else None)
    d_normed = jnp.einsum(
        "cr,dc->rd", d_qkv_t, query_key_value_weight, preferred_element_type=jnp.float32
    )
    d_normed = d_normed + jnp.dot(member.astype(jnp.float32), per_part, precision=HIGH_PRECISION)
    scaled_attn = d_normed * gain_attn
    d_features = (
        d_resid.astype(jnp.float32)
        + inv_attn
        * (scaled_attn - unit_attn * jnp.mean(scaled_attn * unit_attn, axis=-1, keepdims=True))
    ).astype(jnp.bfloat16)
    gain_local = jnp.concatenate(
        [jnp.sum(d_normed * unit_attn, axis=0), jnp.sum(d_normed_ffn * unit_ffn, axis=0)]
    )
    gain_share = 2 * width // seq_size
    gain_block = jnp.pad(
        gain_local.astype(jnp.bfloat16).reshape(seq_size, 1, gain_share),
        ((0, 0), (0, share - 1), (0, 128 - gain_share)),
    )
    middle = late.shape[2] // 2
    late_one = late[:, :, :middle]
    late_two = jnp.concatenate([late[:, :, middle:], gain_block], axis=2)
    if share % 16 == 0:
        late_one, late_two = fold(late_one, late_two)
    else:
        late_one, first_left = as_bits(late_one)
        late_two, second_left = as_bits(late_two)
        for bit in [0, 1] + outer:
            late_one, first_left = halve(late_one, first_left, bit)
            late_two, second_left = halve(late_two, second_left, bit)
    late_sum = jnp.concatenate([late_one, late_two], axis=1)
    grad_gains = late_sum[0, 3 * width : 3 * width + gain_share]
    grad_w_in = one
    grad_w_out = two[:, :width]
    grad_w_down = jnp.concatenate(
        [two[:, c : c + width] for c in range(width, two.shape[1], width)], axis=0
    )
    my_virtual = lax.dynamic_slice_in_dim(virtual, me * share, share, 1)
    virtual_grad = jnp.einsum("pd,sp->ds", my_virtual, d_virt, preferred_element_type=jnp.float32)
    grad_qkv = jnp.concatenate(
        [late_sum[:, :width], late_sum[:, width : 3 * width] + virtual_grad], axis=1
    )
    return (layer_out, d_features, grad_qkv, grad_w_out, grad_w_in, grad_w_down, grad_gains)


def solution(mesh):
    node = P(("groups", "seq"), None)
    flat = P(("groups", "seq"))
    return jax.shard_map(
        on_device,
        mesh=mesh,
        in_specs=(node, P(), P(), P(), P(), P(), P(), node, flat, flat, node),
        out_specs=(node, node, node, node, node, node, flat),
        check_vma=False,
    )
```

```python
import functools
import math

import jax
import jax.numpy as jnp
from jax import lax
from jax.experimental import pallas as pl
from jax.experimental.pallas import tpu as pltpu
from jax.sharding import PartitionSpec as P

HEADS = 16
KT = 4
VN_DEV = 2
CAP = 30.0
EPS = 1e-06
HIGH_PRECISION = lax.Precision.HIGHEST
VMEM_BYTES = 48 * 1024 * 1024


def rms_parts(values):
    inverse = lax.rsqrt(jnp.mean(values * values, axis=-1, keepdims=True) + EPS)
    return (inverse, values * inverse)


def dot_tn(a, b):
    return lax.dot_general(a, b, (((0,), (0,)), ((), ())), preferred_element_type=jnp.float32)


def dot_nt(a, b):
    return lax.dot_general(a, b, (((1,), (1,)), ((), ())), preferred_element_type=jnp.float32)


def dot_nn(a, b):
    return jnp.dot(a, b, preferred_element_type=jnp.float32)


def tile_weights(lists_ref, qkv_ref, virt_ref, t, head_dim):
    count = lists_ref[t, KT]
    query = qkv_ref[lists_ref[t, 0], 0:head_dim, :]
    scale = 1.0 / (math.sqrt(head_dim) * CAP)
    tanhs, weights = [], []
    for j in range(KT):
        keys = qkv_ref[lists_ref[t, j], head_dim : 2 * head_dim, :]
        th = jnp.tanh(dot_tn(keys, query) * scale)
        w = jnp.exp(CAP * th)
        if j:
            w = w * jnp.where(j < count, 1.0, 0.0)
        tanhs.append(th)
        weights.append(w)
    th = jnp.tanh(dot_tn(virt_ref[0], query) * scale)
    tanhs.append(th)
    weights.append(jnp.exp(CAP * th))
    total = jnp.sum(weights[0], axis=0, keepdims=True)
    for w in weights[1:]:
        total = total + jnp.sum(w, axis=0, keepdims=True)
    inverse = 1.0 / total
    return query, tanhs, [w * inverse for w in weights]


def forward_kernel(
    head_dim, slices, size, lists_ref, qkv_ref, virt_ref, heads_ref, out_ref, send, recv
):
    me = lax.axis_index("seq")
    tiles_here = size // slices
    my_head = me // slices
    my_slice = me % slices
    from_slice = me // tiles_here

    def copy(t, head, to):
        return pltpu.make_async_remote_copy(
            src_ref=out_ref.at[t],
            dst_ref=heads_ref.at[head],
            send_sem=send.at[t],
            recv_sem=recv.at[head],
            device_id={"seq": to},
            device_id_type=pl.DeviceIdType.MESH,
        )

    def tile_rows(t):
        _, _, probs = tile_weights(lists_ref, qkv_ref, virt_ref, t, head_dim)
        out = dot_nn(virt_ref[1], probs[KT].astype(jnp.bfloat16))
        for j in range(KT):
            values = qkv_ref[lists_ref[t, j], 2 * head_dim : 3 * head_dim, :]
            out = out + dot_nn(values, probs[j].astype(jnp.bfloat16))
        return out.astype(jnp.bfloat16)

    barrier = pltpu.get_barrier_semaphore()

    def greet(k, carry):
        pl.semaphore_signal(
            barrier,
            inc=1,
            device_id={"seq": lax.rem(me + k, size)},
            device_id_type=pl.DeviceIdType.MESH,
        )
        return carry

    lax.fori_loop(1, size, greet, 0)
    pl.semaphore_wait(barrier, size - 1)

    def body(k, carry):
        pair = [lax.rem(me + 2 * k + 1 + u, tiles_here) for u in range(2)]
        rows = [tile_rows(t) for t in pair]
        for t, values in zip(pair, rows):
            out_ref[t] = values
        for t in pair:
            to = my_slice * tiles_here + t

            @pl.when(to != me)
            def _():
                copy(t, my_head, to).start()

            @pl.when(to == me)
            def _():
                heads_ref[my_head] = out_ref[t]

        return carry

    lax.fori_loop(0, tiles_here // 2, body, 0)

    def arrive(head, carry):
        @pl.when(head * slices + from_slice != me)
        def _():
            copy(0, head, me).wait_recv()

        return carry

    lax.fori_loop(0, HEADS, arrive, 0)

    def leave(t, carry):
        @pl.when(my_slice * tiles_here + t != me)
        def _():
            copy(t, my_head, me).wait_send()

        return carry

    lax.fori_loop(0, tiles_here, leave, 0)


def backward_kernel(
    head_dim, lists_ref, qkv_ref, virt_ref, grad_ref, dq_ref, dkv_ref, dvirt_ref, acc_ref
):
    scale = 1.0 / math.sqrt(head_dim)
    acc_ref[...] = jnp.zeros_like(acc_ref)
    dvirt_ref[...] = jnp.zeros_like(dvirt_ref)

    def body(t, carry):
        query, tanhs, probs = tile_weights(lists_ref, qkv_ref, virt_ref, t, head_dim)
        grad = grad_ref[t]
        dps = []
        for j in range(KT):
            values = qkv_ref[lists_ref[t, j], 2 * head_dim : 3 * head_dim, :]
            dps.append(dot_tn(values, grad))
        dps.append(dot_tn(virt_ref[1], grad))
        inner = jnp.sum(probs[0] * dps[0], axis=0, keepdims=True)
        for j in range(1, KT + 1):
            inner = inner + jnp.sum(probs[j] * dps[j], axis=0, keepdims=True)
        ds = [
            (p * (dp - inner) * (1.0 - th * th) * scale).astype(jnp.bfloat16)
            for p, dp, th in zip(probs, dps, tanhs)
        ]
        pb = [p.astype(jnp.bfloat16) for p in probs]
        dq = dot_nn(virt_ref[0], ds[KT])
        for j in range(KT):
            dq = dq + dot_nn(qkv_ref[lists_ref[t, j], head_dim : 2 * head_dim, :], ds[j])
        dq_ref[t] = dq.astype(jnp.bfloat16)
        for j in range(KT):
            target = lists_ref[t, j]
            acc_ref[target, 0:head_dim, :] += dot_nt(query, ds[j])
            acc_ref[target, head_dim : 2 * head_dim, :] += dot_nt(grad, pb[j])
        dvirt_ref[0:head_dim, :] += dot_nt(query, ds[KT])
        dvirt_ref[head_dim : 2 * head_dim, :] += dot_nt(grad, pb[KT])
        return carry

    lax.fori_loop(0, grad_ref.shape[0], body, 0, unroll=2)
    dkv_ref[...] = acc_ref[...].astype(jnp.bfloat16)


def attention_forward(lists, qkv_all, virt, head_dim, slices):
    tiles_here = lists.shape[0]
    size, _, rows = qkv_all.shape
    pairs = tiles_here * rows * (KT * rows + virt.shape[2])
    vmem = pl.BlockSpec(memory_space=pltpu.VMEM)
    return pl.pallas_call(
        functools.partial(forward_kernel, head_dim, slices, size),
        out_shape=jax.ShapeDtypeStruct((HEADS, head_dim, rows), jnp.bfloat16),
        in_specs=[pl.BlockSpec(memory_space=pltpu.SMEM), vmem, vmem],
        out_specs=vmem,
        scratch_shapes=[
            pltpu.VMEM((tiles_here, head_dim, rows), jnp.bfloat16),
            pltpu.SemaphoreType.DMA((tiles_here,)),
            pltpu.SemaphoreType.DMA((HEADS,)),
        ],
        compiler_params=pltpu.CompilerParams(
            vmem_limit_bytes=VMEM_BYTES, collective_id=1, has_side_effects=True
        ),
        cost_estimate=pl.CostEstimate(
            flops=4 * pairs * head_dim, bytes_accessed=2 * qkv_all.size, transcendentals=2 * pairs
        ),
    )(lists, qkv_all, virt)


def attention_backward(lists, qkv_all, virt, grads, head_dim):
    tiles_here, _, rows = grads.shape
    tiles = qkv_all.shape[0]
    parts = virt.shape[2]
    pairs = tiles_here * rows * (KT * rows + parts)
    vmem = pl.BlockSpec(memory_space=pltpu.VMEM)
    return pl.pallas_call(
        functools.partial(backward_kernel, head_dim),
        out_shape=(
            jax.ShapeDtypeStruct((tiles_here, head_dim, rows), jnp.bfloat16),
            jax.ShapeDtypeStruct((tiles, 2 * head_dim, rows), jnp.bfloat16),
            jax.ShapeDtypeStruct((2 * head_dim, parts), jnp.float32),
        ),
        in_specs=[pl.BlockSpec(memory_space=pltpu.SMEM), vmem, vmem, vmem],
        out_specs=(vmem, vmem, vmem),
        scratch_shapes=[pltpu.VMEM((tiles, 2 * head_dim, rows), jnp.float32)],
        compiler_params=pltpu.CompilerParams(vmem_limit_bytes=VMEM_BYTES),
        cost_estimate=pl.CostEstimate(
            flops=10 * pairs * head_dim, bytes_accessed=6 * qkv_all.size, transcendentals=2 * pairs
        ),
    )(lists, qkv_all, virt, grads)


def all_to_all(blocks):
    return lax.all_to_all(blocks, "seq", split_axis=0, concat_axis=0, tiled=True)


def as_bits(blocks):
    bits = blocks.shape[0].bit_length() - 1
    return blocks.reshape((2,) * bits + blocks.shape[1:]), list(range(bits - 1, -1, -1))


def halve(held, left, bit, after=None):
    size = lax.axis_size("seq")
    mine = (lax.axis_index("seq") // (1 << bit)) % 2
    axis = left.index(bit)
    keep = lax.dynamic_index_in_dim(held, mine, axis, keepdims=False)
    send = lax.dynamic_index_in_dim(held, 1 - mine, axis, keepdims=False)
    got = lax.ppermute(send, "seq", [(i, i ^ (1 << bit)) for i in range(size)])
    if after is not None:
        got, _ = lax.optimization_barrier((got, after))
    total = keep.astype(jnp.float32) + got.astype(jnp.float32)
    rest = [b for b in left if b != bit]
    return (total if not rest else total.astype(jnp.bfloat16)), rest


def exchange_kernel(
    slices, sums_ref, list_ref, qkv_ref, qkv_all_ref, second_ref, first_ref, own_ref, send, recv
):
    size = qkv_all_ref.shape[0]
    me = lax.axis_index("seq")

    def peer(k):
        return lax.rem(me + k, size)

    def each(step):
        def body(k, carry):
            step(k, peer(k))
            return carry

        lax.fori_loop(1, size, body, 0)

    def remote(src, dst, which, k, to):
        return pltpu.make_async_remote_copy(
            src_ref=src,
            dst_ref=dst,
            send_sem=send.at[which, k],
            recv_sem=recv.at[which, k],
            device_id={"seq": to},
            device_id_type=pl.DeviceIdType.MESH,
        )

    def first_copy(k, to):
        return remote(sums_ref.at[to], first_ref.at[me], 0, k, to)

    def second_copy(k, to):
        return remote(own_ref, second_ref.at[me], 1, k, to)

    def head_copy(k, to):
        return remote(qkv_ref.at[to // slices], qkv_all_ref.at[me], 2, k, to)

    barrier = pltpu.get_barrier_semaphore()
    each(
        lambda k, to: pl.semaphore_signal(
            barrier, inc=1, device_id={"seq": to}, device_id_type=pl.DeviceIdType.MESH
        )
    )
    first_ref[me] = sums_ref[me]
    qkv_all_ref[me] = qkv_ref[me // slices]
    pl.semaphore_wait(barrier, size - 1)
    each(lambda k, to: first_copy(k, to).start())
    each(lambda k, to: head_copy(k, to).start())
    each(lambda k, to: first_copy(k, to).wait_recv())
    own_ref[...] = (
        list_ref[...] + jnp.sum(first_ref[...].astype(jnp.float32), axis=0)
    ).astype(own_ref.dtype)
    each(lambda k, to: second_copy(k, to).start())
    second_ref[me] = own_ref[...]
    each(lambda k, to: second_copy(k, to).wait_recv())
    each(lambda k, to: head_copy(k, to).wait_recv())
    each(lambda k, to: first_copy(k, to).wait_send())
    each(lambda k, to: second_copy(k, to).wait_send())
    each(lambda k, to: head_copy(k, to).wait_send())


def exchange(sums, list_rows, qkv_heads, slices):
    size = sums.shape[0]
    vmem = pl.BlockSpec(memory_space=pltpu.VMEM)
    return pl.pallas_call(
        functools.partial(exchange_kernel, slices),
        out_shape=(
            jax.ShapeDtypeStruct((size,) + qkv_heads.shape[1:], qkv_heads.dtype),
            jax.ShapeDtypeStruct(sums.shape, sums.dtype),
        ),
        in_specs=[vmem, vmem, vmem],
        out_specs=(vmem, vmem),
        scratch_shapes=[
            pltpu.VMEM(sums.shape, sums.dtype),
            pltpu.VMEM(sums.shape[1:], sums.dtype),
            pltpu.SemaphoreType.DMA((3, size)),
            pltpu.SemaphoreType.DMA((3, size)),
        ],
        compiler_params=pltpu.CompilerParams(
            vmem_limit_bytes=VMEM_BYTES, collective_id=0, has_side_effects=True
        ),
        cost_estimate=pl.CostEstimate(
            flops=sums.size, bytes_accessed=4 * size * qkv_heads[0].size, transcendentals=0
        ),
    )(sums, list_rows, qkv_heads)


def fold_kernel(orders, bits, *refs):
    me = lax.axis_index("seq")
    streams = range(len(orders))
    count = len(orders)
    inputs, outputs = refs[:count], refs[count : 2 * count]
    scratch = list(refs[2 * count : -2])
    send, recv = refs[-2:]
    landing = [[scratch.pop(0) for _ in order] for order in orders]
    held = [[scratch.pop(0) for _ in order[1:]] for order in orders]

    def partner(bit):
        return me + (1 << bit) * (1 - 2 * ((me // (1 << bit)) % 2))

    def half(stream, step, theirs):
        bit = orders[stream][step]
        left = sorted(orders[stream][step:], reverse=True)
        mine = (me // (1 << bit)) % 2
        index = (slice(None),) * left.index(bit) + (1 - mine if theirs else mine,)
        return (inputs[stream] if step == 0 else held[stream][step - 1]), index

    def copy(stream, step):
        source, index = half(stream, step, True)
        return pltpu.make_async_remote_copy(
            src_ref=source.at[index],
            dst_ref=landing[stream][step],
            send_sem=send.at[stream, step],
            recv_sem=recv.at[stream, step],
            device_id={"seq": partner(orders[stream][step])},
            device_id_type=pl.DeviceIdType.MESH,
        )

    barrier = pltpu.get_barrier_semaphore()
    for bit in range(bits):
        pl.semaphore_signal(
            barrier,
            inc=1,
            device_id={"seq": partner(bit)},
            device_id_type=pl.DeviceIdType.MESH,
        )
    pl.semaphore_wait(barrier, bits)
    for stream in streams:
        copy(stream, 0).start()
    for step in range(bits):
        for stream in streams:
            last = len(orders[stream]) - 1
            if step > last:
                continue
            copy(stream, step).wait_recv()
            source, index = half(stream, step, False)
            total = source[index].astype(jnp.float32) + landing[stream][step][...].astype(
                jnp.float32
            )
            if step == last:
                outputs[stream][...] = total
            else:
                held[stream][step][...] = total.astype(jnp.bfloat16)
                copy(stream, step + 1).start()
    for stream in streams:
        for step in range(len(orders[stream])):
            copy(stream, step).wait_send()


def fold(arrays, orders, bits):
    count = len(arrays)
    vmem = pl.BlockSpec(memory_space=pltpu.VMEM)
    tails = [array.shape[len(order) :] for array, order in zip(arrays, orders)]
    landing, held = [], []
    for tail, order in zip(tails, orders):
        shapes = [(2,) * (len(order) - 1 - step) + tail for step in range(len(order))]
        landing += [pltpu.VMEM(shape, jnp.bfloat16) for shape in shapes]
        held += [pltpu.VMEM(shape, jnp.bfloat16) for shape in shapes[:-1]]
    return pl.pallas_call(
        functools.partial(fold_kernel, orders, bits),
        out_shape=tuple(jax.ShapeDtypeStruct(tail, jnp.float32) for tail in tails),
        in_specs=[vmem] * count,
        out_specs=(vmem,) * count,
        scratch_shapes=landing
        + held
        + [pltpu.SemaphoreType.DMA((count, bits)), pltpu.SemaphoreType.DMA((count, bits))],
        compiler_params=pltpu.CompilerParams(
            vmem_limit_bytes=VMEM_BYTES, collective_id=2, has_side_effects=True
        ),
        cost_estimate=pl.CostEstimate(
            flops=arrays[0].size,
            bytes_accessed=8 * sum(array.size for array in arrays),
            transcendentals=0,
        ),
    )(*arrays)


def on_device(
    features,
    gain_attn,
    gain_ffn,
    query_key_value_weight,
    w_out,
    w_in,
    w_down,
    tile_lists,
    tile_count,
    partition,
    grad_out,
):
    rows, width = features.shape
    head_dim = width // HEADS
    hidden_units = w_down.shape[0]
    seq_size = lax.axis_size("seq")
    me = lax.axis_index("seq")
    parts = VN_DEV * seq_size
    slices = seq_size // HEADS
    my_head = me // slices
    my_slice = me % slices
    tiles_here = seq_size // slices
    slice_of_me = me // tiles_here

    x_f = features.astype(jnp.float32)
    inv_attn, unit_attn = rms_parts(x_f)
    normed = (unit_attn * gain_attn).astype(jnp.bfloat16)
    member = (partition[:, None] == jnp.arange(parts, dtype=jnp.int32)[None, :]).astype(
        jnp.bfloat16
    )
    part_sums = jnp.einsum("rp,rd->pd", member, normed, preferred_element_type=jnp.float32)
    part_counts = jnp.sum(member.astype(jnp.float32), axis=0)
    lanes = 128
    sum_rows = VN_DEV * width // lanes
    list_at = sum_rows + VN_DEV
    block_rows = -(-(list_at + 1) // 16) * 16
    sums = jnp.concatenate(
        [
            part_sums.reshape(seq_size, sum_rows, lanes),
            jnp.broadcast_to(
                part_counts.reshape(seq_size, VN_DEV, 1), (seq_size, VN_DEV, lanes)
            ),
            jnp.zeros((seq_size, block_rows - list_at, lanes), jnp.float32),
        ],
        axis=1,
    ).astype(jnp.bfloat16)
    list_rows = jnp.pad(
        jnp.concatenate([tile_lists[0], tile_count]).astype(jnp.float32)[None],
        ((list_at, block_rows - list_at - 1), (0, lanes - KT - 1)),
    )
    qkv = jnp.dot(normed, query_key_value_weight, preferred_element_type=jnp.float32)
    qkv_t = lax.optimization_barrier(qkv.astype(jnp.bfloat16)).T
    qkv_heads = jnp.transpose(qkv_t.reshape(3, HEADS, head_dim, rows), (1, 0, 2, 3)).reshape(
        HEADS, 3 * head_dim, rows
    )
    qkv_all, second = exchange(sums, list_rows, qkv_heads, slices)
    second = second.astype(jnp.float32)
    totals = second[:, :sum_rows].reshape(parts, width)
    counts = second[:, sum_rows:list_at, :1].reshape(parts, 1)
    lists_all = second[:, list_at, : KT + 1].astype(jnp.int32)
    part_mean = totals / counts
    inv_vn, unit_vn = rms_parts(part_mean)
    virtual = unit_vn.astype(jnp.bfloat16)

    lists = lax.dynamic_slice_in_dim(lists_all, my_slice * tiles_here, tiles_here, 0)
    weight_heads = query_key_value_weight.reshape(width, 3, HEADS, head_dim)
    my_columns = lax.dynamic_index_in_dim(weight_heads, my_head, 2, keepdims=False)[:, 1:]
    virt = jnp.einsum(
        "dke,pd->kep", my_columns, virtual, preferred_element_type=jnp.float32
    ).astype(jnp.bfloat16)

    def spread(local):
        if slices == 1:
            return local
        empty = jnp.zeros((seq_size,) + local.shape[1:], local.dtype)
        return lax.dynamic_update_slice_in_dim(empty, local, my_slice * tiles_here, 0)

    def pick_slice(received):
        split = received.reshape((HEADS, slices) + received.shape[1:])
        return lax.dynamic_index_in_dim(split, slice_of_me, 1, keepdims=False)

    attn_out_t = attention_forward(lists, qkv_all, virt, head_dim, slices).reshape(width, rows)

    mixed = jnp.einsum("dr,de->re", attn_out_t, w_out, preferred_element_type=jnp.float32)
    resid = (x_f + mixed).astype(jnp.bfloat16)
    res_f = resid.astype(jnp.float32)
    inv_ffn, unit_ffn = rms_parts(res_f)
    normed_ffn = (unit_ffn * gain_ffn).astype(jnp.bfloat16)
    gate_up = jnp.dot(normed_ffn, w_in, preferred_element_type=jnp.float32)
    gate_proj = gate_up[:, :hidden_units]
    up_proj = gate_up[:, hidden_units:]
    sigmoid_gate = jax.nn.sigmoid(gate_proj)
    activated = gate_proj * sigmoid_gate
    hidden = (activated * up_proj).astype(jnp.bfloat16)
    layer_out = (res_f + jnp.dot(hidden, w_down, preferred_element_type=jnp.float32)).astype(
        jnp.bfloat16
    )
    d_hidden = jnp.einsum("rd,fd->rf", grad_out, w_down, preferred_element_type=jnp.float32)
    d_gate = d_hidden * up_proj * sigmoid_gate * (1.0 + gate_proj * (1.0 - sigmoid_gate))
    d_up = d_hidden * activated
    d_both = jnp.concatenate([d_gate, d_up], axis=1).astype(jnp.bfloat16)
    d_normed_ffn = jnp.einsum("rf,df->rd", d_both, w_in, preferred_element_type=jnp.float32)
    scaled_ffn = d_normed_ffn * gain_ffn
    d_resid = (
        grad_out.astype(jnp.float32)
        + inv_ffn
        * (scaled_ffn - unit_ffn * jnp.mean(scaled_ffn * unit_ffn, axis=-1, keepdims=True))
    ).astype(jnp.bfloat16)
    d_attn_t = jnp.einsum("de,re->dr", w_out, d_resid, preferred_element_type=jnp.float32).astype(
        jnp.bfloat16
    )
    d_heads = jnp.broadcast_to(
        d_attn_t.reshape(HEADS, 1, head_dim, rows), (HEADS, slices, head_dim, rows)
    ).reshape(seq_size, head_dim, rows)
    grads = lax.dynamic_slice_in_dim(all_to_all(d_heads), my_slice * tiles_here, tiles_here, 0)

    share = width // seq_size
    grad_out_local = jnp.einsum("dr,re->de", attn_out_t, d_resid, preferred_element_type=jnp.float32)
    grad_in_local = jnp.einsum("rd,rf->df", normed_ffn, d_both, preferred_element_type=jnp.float32)
    grad_down_local = jnp.einsum("rf,rd->fd", hidden, grad_out, preferred_element_type=jnp.float32)
    down_blocks = grad_down_local.astype(jnp.bfloat16).reshape(seq_size, -1, share, width)
    bits = seq_size.bit_length() - 1
    outer = list(range(2, bits))
    one, one_left = as_bits(grad_in_local.astype(jnp.bfloat16).reshape(seq_size, share, -1))
    two, two_left = as_bits(
        jnp.concatenate(
            [grad_out_local.astype(jnp.bfloat16).reshape(seq_size, share, -1)]
            + [down_blocks[:, i] for i in range(down_blocks.shape[1])],
            axis=2,
        )
    )
    one, one_left = halve(one, one_left, 0)
    two, two_left = halve(two, two_left, 0)
    grads, one, two = lax.optimization_barrier((grads, one, two))
    one, one_left = halve(one, one_left, 1)
    two, two_left = halve(two, two_left, outer[0])
    one_order = outer
    two_order = outer[1:] + [1]

    dq, dkv, dvirt = attention_backward(lists, qkv_all, virt, grads, head_dim)
    dq, one, two = lax.optimization_barrier((dq, one, two))
    virt_rows = 2 * head_dim * parts // rows
    back_send = jnp.concatenate(
        [
            spread(dq),
            dkv,
            jnp.broadcast_to(
                dvirt.astype(jnp.bfloat16).reshape(virt_rows, rows), (seq_size, virt_rows, rows)
            ),
        ],
        axis=1,
    )
    back = all_to_all(back_send)
    dq_t = pick_slice(back[:, :head_dim])
    rest = back[:, head_dim:]
    if slices > 1:
        rest = jnp.sum(
            rest.reshape(HEADS, slices, -1, rows).astype(jnp.float32), axis=1
        ).astype(jnp.bfloat16)
    d_qkv_t = jnp.concatenate(
        [dq_t, rest[:, :head_dim], rest[:, head_dim : 2 * head_dim]], axis=0
    ).reshape(3 * width, rows)
    d_virt = (
        rest[:, 2 * head_dim :]
        .reshape(HEADS, 2, head_dim, parts)
        .transpose(1, 0, 2, 3)
        .reshape(2 * width, parts)
    )
    d_virtual = jnp.einsum(
        "sp,ds->pd", d_virt, query_key_value_weight[:, width:], preferred_element_type=jnp.float32
    )
    inner_vn = jnp.mean(d_virtual * unit_vn, axis=-1, keepdims=True)
    per_part = inv_vn * (d_virtual - unit_vn * inner_vn) / counts
    grad_qkv_local = jnp.einsum("rd,cr->dc", normed, d_qkv_t, preferred_element_type=jnp.float32)
    late = grad_qkv_local.astype(jnp.bfloat16).reshape(seq_size, share, -1)
    for bit in one_order[:-1]:
        one, one_left = halve(one, one_left, bit, late)
    for bit in two_order[:-1]:
        two, two_left = halve(two, two_left, bit, late)
    d_normed = jnp.einsum(
        "cr,dc->rd", d_qkv_t, query_key_value_weight, preferred_element_type=jnp.float32
    )
    d_normed = d_normed + jnp.dot(member.astype(jnp.float32), per_part, precision=HIGH_PRECISION)
    scaled_attn = d_normed * gain_attn
    d_features = (
        d_resid.astype(jnp.float32)
        + inv_attn
        * (scaled_attn - unit_attn * jnp.mean(scaled_attn * unit_attn, axis=-1, keepdims=True))
    ).astype(jnp.bfloat16)
    gain_local = jnp.concatenate(
        [jnp.sum(d_normed * unit_attn, axis=0), jnp.sum(d_normed_ffn * unit_ffn, axis=0)]
    )
    gain_share = 2 * width // seq_size
    gain_block = jnp.pad(
        gain_local.astype(jnp.bfloat16).reshape(seq_size, 1, gain_share),
        ((0, 0), (0, share - 1), (0, 128 - gain_share)),
    )
    middle = late.shape[2] // 2
    late_one = late[:, :, :middle]
    late_two = jnp.concatenate([late[:, :, middle:], gain_block], axis=2)
    late_one, first_left = as_bits(late_one)
    late_two, second_left = as_bits(late_two)
    if share % 16 == 0:
        one, two, late_one, late_two = fold(
            [one, two, late_one, late_two],
            [one_left, two_left, [0, 1] + outer, [0] + outer + [1]],
            bits,
        )
    else:
        one, one_left = halve(one, one_left, one_left[0])
        two, two_left = halve(two, two_left, two_left[0])
        for bit in [0, 1] + outer:
            late_one, first_left = halve(late_one, first_left, bit)
            late_two, second_left = halve(late_two, second_left, bit)
    late_sum = jnp.concatenate([late_one, late_two], axis=1)
    grad_gains = late_sum[0, 3 * width : 3 * width + gain_share]
    grad_w_in = one
    grad_w_out = two[:, :width]
    grad_w_down = jnp.concatenate(
        [two[:, c : c + width] for c in range(width, two.shape[1], width)], axis=0
    )
    my_virtual = lax.dynamic_slice_in_dim(virtual, me * share, share, 1)
    virtual_grad = jnp.einsum("pd,sp->ds", my_virtual, d_virt, preferred_element_type=jnp.float32)
    grad_qkv = jnp.concatenate(
        [late_sum[:, :width], late_sum[:, width : 3 * width] + virtual_grad], axis=1
    )
    return (layer_out, d_features, grad_qkv, grad_w_out, grad_w_in, grad_w_down, grad_gains)


def solution(mesh):
    node = P(("groups", "seq"), None)
    flat = P(("groups", "seq"))
    return jax.shard_map(
        on_device,
        mesh=mesh,
        in_specs=(node, P(), P(), P(), P(), P(), P(), node, flat, flat, node),
        out_specs=(node, node, node, node, node, node, flat),
        check_vma=False,
    )
```

```python
import functools
import math

import jax
import jax.numpy as jnp
from jax import lax
from jax.experimental import pallas as pl
from jax.experimental.pallas import tpu as pltpu
from jax.sharding import PartitionSpec as P

HEADS = 16
KT = 4
VN_DEV = 2
CAP = 30.0
EPS = 1e-06
HIGH_PRECISION = lax.Precision.HIGHEST
VMEM_BYTES = 48 * 1024 * 1024


def rms_parts(values):
    inverse = lax.rsqrt(jnp.mean(values * values, axis=-1, keepdims=True) + EPS)
    return (inverse, values * inverse)


def dot_tn(a, b):
    return lax.dot_general(a, b, (((0,), (0,)), ((), ())), preferred_element_type=jnp.float32)


def dot_nt(a, b):
    return lax.dot_general(a, b, (((1,), (1,)), ((), ())), preferred_element_type=jnp.float32)


def dot_nn(a, b):
    return jnp.dot(a, b, preferred_element_type=jnp.float32)


def tile_weights(lists_ref, qkv_ref, virt_ref, t, head_dim):
    count = lists_ref[t, KT]
    query = qkv_ref[lists_ref[t, 0], 0:head_dim, :]
    scale = 1.0 / (math.sqrt(head_dim) * CAP)
    tanhs, weights = [], []
    for j in range(KT):
        keys = qkv_ref[lists_ref[t, j], head_dim : 2 * head_dim, :]
        th = jnp.tanh(dot_tn(keys, query) * scale)
        w = jnp.exp(CAP * th)
        if j:
            w = w * jnp.where(j < count, 1.0, 0.0)
        tanhs.append(th)
        weights.append(w)
    th = jnp.tanh(dot_tn(virt_ref[0], query) * scale)
    tanhs.append(th)
    weights.append(jnp.exp(CAP * th))
    total = jnp.sum(weights[0], axis=0, keepdims=True)
    for w in weights[1:]:
        total = total + jnp.sum(w, axis=0, keepdims=True)
    inverse = 1.0 / total
    return query, tanhs, [w * inverse for w in weights]


def forward_kernel(
    head_dim, slices, size, lists_ref, qkv_ref, virt_ref, heads_ref, out_ref, send, recv
):
    me = lax.axis_index("seq")
    tiles_here = size // slices
    my_head = me // slices
    my_slice = me % slices
    from_slice = me // tiles_here

    def copy(t, head, to):
        return pltpu.make_async_remote_copy(
            src_ref=out_ref.at[t],
            dst_ref=heads_ref.at[head],
            send_sem=send.at[t],
            recv_sem=recv.at[head],
            device_id={"seq": to},
            device_id_type=pl.DeviceIdType.MESH,
        )

    def tile_rows(t):
        _, _, probs = tile_weights(lists_ref, qkv_ref, virt_ref, t, head_dim)
        out = dot_nn(virt_ref[1], probs[KT].astype(jnp.bfloat16))
        for j in range(KT):
            values = qkv_ref[lists_ref[t, j], 2 * head_dim : 3 * head_dim, :]
            out = out + dot_nn(values, probs[j].astype(jnp.bfloat16))
        return out.astype(jnp.bfloat16)

    barrier = pltpu.get_barrier_semaphore()

    def greet(k, carry):
        pl.semaphore_signal(
            barrier,
            inc=1,
            device_id={"seq": lax.rem(me + k, size)},
            device_id_type=pl.DeviceIdType.MESH,
        )
        return carry

    lax.fori_loop(1, size, greet, 0)
    pl.semaphore_wait(barrier, size - 1)

    def body(k, carry):
        pair = [lax.rem(me + 2 * k + 1 + u, tiles_here) for u in range(2)]
        rows = [tile_rows(t) for t in pair]
        for t, values in zip(pair, rows):
            out_ref[t] = values
        for t in pair:
            to = my_slice * tiles_here + t

            @pl.when(to != me)
            def _():
                copy(t, my_head, to).start()

            @pl.when(to == me)
            def _():
                heads_ref[my_head] = out_ref[t]

        return carry

    lax.fori_loop(0, tiles_here // 2, body, 0)

    def arrive(head, carry):
        @pl.when(head * slices + from_slice != me)
        def _():
            copy(0, head, me).wait_recv()

        return carry

    lax.fori_loop(0, HEADS, arrive, 0)

    def leave(t, carry):
        @pl.when(my_slice * tiles_here + t != me)
        def _():
            copy(t, my_head, me).wait_send()

        return carry

    lax.fori_loop(0, tiles_here, leave, 0)


def backward_kernel(
    head_dim, lists_ref, qkv_ref, virt_ref, grad_ref, dq_ref, dkv_ref, dvirt_ref, acc_ref
):
    scale = 1.0 / math.sqrt(head_dim)
    acc_ref[...] = jnp.zeros_like(acc_ref)
    dvirt_ref[...] = jnp.zeros_like(dvirt_ref)

    def body(t, carry):
        query, tanhs, probs = tile_weights(lists_ref, qkv_ref, virt_ref, t, head_dim)
        grad = grad_ref[t]
        dps = []
        for j in range(KT):
            values = qkv_ref[lists_ref[t, j], 2 * head_dim : 3 * head_dim, :]
            dps.append(dot_tn(values, grad))
        dps.append(dot_tn(virt_ref[1], grad))
        inner = jnp.sum(probs[0] * dps[0], axis=0, keepdims=True)
        for j in range(1, KT + 1):
            inner = inner + jnp.sum(probs[j] * dps[j], axis=0, keepdims=True)
        ds = [
            (p * (dp - inner) * (1.0 - th * th) * scale).astype(jnp.bfloat16)
            for p, dp, th in zip(probs, dps, tanhs)
        ]
        pb = [p.astype(jnp.bfloat16) for p in probs]
        dq = dot_nn(virt_ref[0], ds[KT])
        for j in range(KT):
            dq = dq + dot_nn(qkv_ref[lists_ref[t, j], head_dim : 2 * head_dim, :], ds[j])
        dq_ref[t] = dq.astype(jnp.bfloat16)
        for j in range(KT):
            target = lists_ref[t, j]
            acc_ref[target, 0:head_dim, :] += dot_nt(query, ds[j])
            acc_ref[target, head_dim : 2 * head_dim, :] += dot_nt(grad, pb[j])
        dvirt_ref[0:head_dim, :] += dot_nt(query, ds[KT])
        dvirt_ref[head_dim : 2 * head_dim, :] += dot_nt(grad, pb[KT])
        return carry

    lax.fori_loop(0, grad_ref.shape[0], body, 0, unroll=2)
    dkv_ref[...] = acc_ref[...].astype(jnp.bfloat16)


def attention_forward(lists, qkv_all, virt, head_dim, slices):
    tiles_here = lists.shape[0]
    size, _, rows = qkv_all.shape
    pairs = tiles_here * rows * (KT * rows + virt.shape[2])
    vmem = pl.BlockSpec(memory_space=pltpu.VMEM)
    return pl.pallas_call(
        functools.partial(forward_kernel, head_dim, slices, size),
        out_shape=jax.ShapeDtypeStruct((HEADS, head_dim, rows), jnp.bfloat16),
        in_specs=[pl.BlockSpec(memory_space=pltpu.SMEM), vmem, vmem],
        out_specs=vmem,
        scratch_shapes=[
            pltpu.VMEM((tiles_here, head_dim, rows), jnp.bfloat16),
            pltpu.SemaphoreType.DMA((tiles_here,)),
            pltpu.SemaphoreType.DMA((HEADS,)),
        ],
        compiler_params=pltpu.CompilerParams(
            vmem_limit_bytes=VMEM_BYTES, collective_id=1, has_side_effects=True
        ),
        cost_estimate=pl.CostEstimate(
            flops=4 * pairs * head_dim, bytes_accessed=2 * qkv_all.size, transcendentals=2 * pairs
        ),
    )(lists, qkv_all, virt)


def attention_backward(lists, qkv_all, virt, grads, head_dim):
    tiles_here, _, rows = grads.shape
    tiles = qkv_all.shape[0]
    parts = virt.shape[2]
    pairs = tiles_here * rows * (KT * rows + parts)
    vmem = pl.BlockSpec(memory_space=pltpu.VMEM)
    return pl.pallas_call(
        functools.partial(backward_kernel, head_dim),
        out_shape=(
            jax.ShapeDtypeStruct((tiles_here, head_dim, rows), jnp.bfloat16),
            jax.ShapeDtypeStruct((tiles, 2 * head_dim, rows), jnp.bfloat16),
            jax.ShapeDtypeStruct((2 * head_dim, parts), jnp.float32),
        ),
        in_specs=[pl.BlockSpec(memory_space=pltpu.SMEM), vmem, vmem, vmem],
        out_specs=(vmem, vmem, vmem),
        scratch_shapes=[pltpu.VMEM((tiles, 2 * head_dim, rows), jnp.float32)],
        compiler_params=pltpu.CompilerParams(vmem_limit_bytes=VMEM_BYTES),
        cost_estimate=pl.CostEstimate(
            flops=10 * pairs * head_dim, bytes_accessed=6 * qkv_all.size, transcendentals=2 * pairs
        ),
    )(lists, qkv_all, virt, grads)


def all_to_all(blocks):
    return lax.all_to_all(blocks, "seq", split_axis=0, concat_axis=0, tiled=True)


def as_bits(blocks):
    bits = blocks.shape[0].bit_length() - 1
    return blocks.reshape((2,) * bits + blocks.shape[1:]), list(range(bits - 1, -1, -1))


def halve(held, left, bit, after=None):
    size = lax.axis_size("seq")
    mine = (lax.axis_index("seq") // (1 << bit)) % 2
    axis = left.index(bit)
    keep = lax.dynamic_index_in_dim(held, mine, axis, keepdims=False)
    send = lax.dynamic_index_in_dim(held, 1 - mine, axis, keepdims=False)
    got = lax.ppermute(send, "seq", [(i, i ^ (1 << bit)) for i in range(size)])
    if after is not None:
        got, _ = lax.optimization_barrier((got, after))
    total = keep.astype(jnp.float32) + got.astype(jnp.float32)
    rest = [b for b in left if b != bit]
    return (total if not rest else total.astype(jnp.bfloat16)), rest


def exchange_kernel(
    slices, sums_ref, list_ref, qkv_ref, qkv_all_ref, second_ref, first_ref, own_ref, send, recv
):
    size = qkv_all_ref.shape[0]
    me = lax.axis_index("seq")

    def peer(k):
        return lax.rem(me + k, size)

    def each(step):
        def body(k, carry):
            step(k, peer(k))
            return carry

        lax.fori_loop(1, size, body, 0)

    def remote(src, dst, which, k, to):
        return pltpu.make_async_remote_copy(
            src_ref=src,
            dst_ref=dst,
            send_sem=send.at[which, k],
            recv_sem=recv.at[which, k],
            device_id={"seq": to},
            device_id_type=pl.DeviceIdType.MESH,
        )

    def first_copy(k, to):
        return remote(sums_ref.at[to], first_ref.at[me], 0, k, to)

    def second_copy(k, to):
        return remote(own_ref, second_ref.at[me], 1, k, to)

    def head_copy(k, to):
        return remote(qkv_ref.at[to // slices], qkv_all_ref.at[me], 2, k, to)

    barrier = pltpu.get_barrier_semaphore()
    each(
        lambda k, to: pl.semaphore_signal(
            barrier, inc=1, device_id={"seq": to}, device_id_type=pl.DeviceIdType.MESH
        )
    )
    first_ref[me] = sums_ref[me]
    qkv_all_ref[me] = qkv_ref[me // slices]
    pl.semaphore_wait(barrier, size - 1)
    each(lambda k, to: first_copy(k, to).start())
    each(lambda k, to: head_copy(k, to).start())
    each(lambda k, to: first_copy(k, to).wait_recv())
    own_ref[...] = (
        list_ref[...] + jnp.sum(first_ref[...].astype(jnp.float32), axis=0)
    ).astype(own_ref.dtype)
    each(lambda k, to: second_copy(k, to).start())
    second_ref[me] = own_ref[...]
    each(lambda k, to: second_copy(k, to).wait_recv())
    each(lambda k, to: head_copy(k, to).wait_recv())
    each(lambda k, to: first_copy(k, to).wait_send())
    each(lambda k, to: second_copy(k, to).wait_send())
    each(lambda k, to: head_copy(k, to).wait_send())


def exchange(sums, list_rows, qkv_heads, slices):
    size = sums.shape[0]
    vmem = pl.BlockSpec(memory_space=pltpu.VMEM)
    return pl.pallas_call(
        functools.partial(exchange_kernel, slices),
        out_shape=(
            jax.ShapeDtypeStruct((size,) + qkv_heads.shape[1:], qkv_heads.dtype),
            jax.ShapeDtypeStruct(sums.shape, sums.dtype),
        ),
        in_specs=[vmem, vmem, vmem],
        out_specs=(vmem, vmem),
        scratch_shapes=[
            pltpu.VMEM(sums.shape, sums.dtype),
            pltpu.VMEM(sums.shape[1:], sums.dtype),
            pltpu.SemaphoreType.DMA((3, size)),
            pltpu.SemaphoreType.DMA((3, size)),
        ],
        compiler_params=pltpu.CompilerParams(
            vmem_limit_bytes=VMEM_BYTES, collective_id=0, has_side_effects=True
        ),
        cost_estimate=pl.CostEstimate(
            flops=sums.size, bytes_accessed=4 * size * qkv_heads[0].size, transcendentals=0
        ),
    )(sums, list_rows, qkv_heads)


def fold_kernel(orders, bits, *refs):
    me = lax.axis_index("seq")
    streams = range(len(orders))
    count = len(orders)
    inputs, outputs = refs[:count], refs[count : 2 * count]
    scratch = list(refs[2 * count : -2])
    send, recv = refs[-2:]
    landing = [[scratch.pop(0) for _ in order] for order in orders]
    held = [[scratch.pop(0) for _ in order[1:]] for order in orders]

    def partner(bit):
        return me + (1 << bit) * (1 - 2 * ((me // (1 << bit)) % 2))

    def half(stream, step, theirs):
        bit = orders[stream][step]
        left = sorted(orders[stream][step:], reverse=True)
        mine = (me // (1 << bit)) % 2
        index = (slice(None),) * left.index(bit) + (1 - mine if theirs else mine,)
        return (inputs[stream] if step == 0 else held[stream][step - 1]), index

    def copy(stream, step):
        source, index = half(stream, step, True)
        return pltpu.make_async_remote_copy(
            src_ref=source.at[index],
            dst_ref=landing[stream][step],
            send_sem=send.at[stream, step],
            recv_sem=recv.at[stream, step],
            device_id={"seq": partner(orders[stream][step])},
            device_id_type=pl.DeviceIdType.MESH,
        )

    barrier = pltpu.get_barrier_semaphore()
    for bit in range(bits):
        pl.semaphore_signal(
            barrier,
            inc=1,
            device_id={"seq": partner(bit)},
            device_id_type=pl.DeviceIdType.MESH,
        )
    pl.semaphore_wait(barrier, bits)
    for stream in streams:
        copy(stream, 0).start()
    for step in range(bits):
        for stream in streams:
            last = len(orders[stream]) - 1
            if step > last:
                continue
            copy(stream, step).wait_recv()
            source, index = half(stream, step, False)
            total = source[index].astype(jnp.float32) + landing[stream][step][...].astype(
                jnp.float32
            )
            if step == last:
                outputs[stream][...] = total
            else:
                held[stream][step][...] = total.astype(jnp.bfloat16)
                copy(stream, step + 1).start()
    for stream in streams:
        for step in range(len(orders[stream])):
            copy(stream, step).wait_send()


def fold(arrays, orders, bits):
    count = len(arrays)
    vmem = pl.BlockSpec(memory_space=pltpu.VMEM)
    tails = [array.shape[len(order) :] for array, order in zip(arrays, orders)]
    landing, held = [], []
    for tail, order in zip(tails, orders):
        shapes = [(2,) * (len(order) - 1 - step) + tail for step in range(len(order))]
        landing += [pltpu.VMEM(shape, jnp.bfloat16) for shape in shapes]
        held += [pltpu.VMEM(shape, jnp.bfloat16) for shape in shapes[:-1]]
    return pl.pallas_call(
        functools.partial(fold_kernel, orders, bits),
        out_shape=tuple(jax.ShapeDtypeStruct(tail, jnp.float32) for tail in tails),
        in_specs=[vmem] * count,
        out_specs=(vmem,) * count,
        scratch_shapes=landing
        + held
        + [pltpu.SemaphoreType.DMA((count, bits)), pltpu.SemaphoreType.DMA((count, bits))],
        compiler_params=pltpu.CompilerParams(
            vmem_limit_bytes=VMEM_BYTES, collective_id=2, has_side_effects=True
        ),
        cost_estimate=pl.CostEstimate(
            flops=arrays[0].size,
            bytes_accessed=8 * sum(array.size for array in arrays),
            transcendentals=0,
        ),
    )(*arrays)


def on_device(
    features,
    gain_attn,
    gain_ffn,
    query_key_value_weight,
    w_out,
    w_in,
    w_down,
    tile_lists,
    tile_count,
    partition,
    grad_out,
):
    rows, width = features.shape
    head_dim = width // HEADS
    hidden_units = w_down.shape[0]
    seq_size = lax.axis_size("seq")
    me = lax.axis_index("seq")
    parts = VN_DEV * seq_size
    slices = seq_size // HEADS
    my_head = me // slices
    my_slice = me % slices
    tiles_here = seq_size // slices
    slice_of_me = me // tiles_here

    x_f = features.astype(jnp.float32)
    inv_attn, unit_attn = rms_parts(x_f)
    normed = (unit_attn * gain_attn).astype(jnp.bfloat16)
    member = (partition[:, None] == jnp.arange(parts, dtype=jnp.int32)[None, :]).astype(
        jnp.bfloat16
    )
    part_sums = jnp.einsum("rp,rd->pd", member, normed, preferred_element_type=jnp.float32)
    part_counts = jnp.sum(member.astype(jnp.float32), axis=0)
    lanes = 128
    sum_rows = VN_DEV * width // lanes
    list_at = sum_rows + VN_DEV
    block_rows = -(-(list_at + 1) // 16) * 16
    sums = jnp.concatenate(
        [
            part_sums.reshape(seq_size, sum_rows, lanes),
            jnp.broadcast_to(
                part_counts.reshape(seq_size, VN_DEV, 1), (seq_size, VN_DEV, lanes)
            ),
            jnp.zeros((seq_size, block_rows - list_at, lanes), jnp.float32),
        ],
        axis=1,
    ).astype(jnp.bfloat16)
    list_rows = jnp.pad(
        jnp.concatenate([tile_lists[0], tile_count]).astype(jnp.float32)[None],
        ((list_at, block_rows - list_at - 1), (0, lanes - KT - 1)),
    )
    qkv = jnp.dot(normed, query_key_value_weight, preferred_element_type=jnp.float32)
    qkv_t = lax.optimization_barrier(qkv.astype(jnp.bfloat16)).T
    qkv_heads = jnp.transpose(qkv_t.reshape(3, HEADS, head_dim, rows), (1, 0, 2, 3)).reshape(
        HEADS, 3 * head_dim, rows
    )
    qkv_all, second = exchange(sums, list_rows, qkv_heads, slices)
    second = second.astype(jnp.float32)
    totals = second[:, :sum_rows].reshape(parts, width)
    counts = second[:, sum_rows:list_at, :1].reshape(parts, 1)
    lists_all = second[:, list_at, : KT + 1].astype(jnp.int32)
    part_mean = totals / counts
    inv_vn, unit_vn = rms_parts(part_mean)
    virtual = unit_vn.astype(jnp.bfloat16)

    lists = lax.dynamic_slice_in_dim(lists_all, my_slice * tiles_here, tiles_here, 0)
    weight_heads = query_key_value_weight.reshape(width, 3, HEADS, head_dim)
    my_columns = lax.dynamic_index_in_dim(weight_heads, my_head, 2, keepdims=False)[:, 1:]
    virt = jnp.einsum(
        "dke,pd->kep", my_columns, virtual, preferred_element_type=jnp.float32
    ).astype(jnp.bfloat16)

    def spread(local):
        if slices == 1:
            return local
        empty = jnp.zeros((seq_size,) + local.shape[1:], local.dtype)
        return lax.dynamic_update_slice_in_dim(empty, local, my_slice * tiles_here, 0)

    def pick_slice(received):
        split = received.reshape((HEADS, slices) + received.shape[1:])
        return lax.dynamic_index_in_dim(split, slice_of_me, 1, keepdims=False)

    attn_out_t = attention_forward(lists, qkv_all, virt, head_dim, slices).reshape(width, rows)

    mixed = jnp.einsum("dr,de->re", attn_out_t, w_out, preferred_element_type=jnp.float32)
    resid = (x_f + mixed).astype(jnp.bfloat16)
    res_f = resid.astype(jnp.float32)
    inv_ffn, unit_ffn = rms_parts(res_f)
    normed_ffn = (unit_ffn * gain_ffn).astype(jnp.bfloat16)
    gate_up = jnp.dot(normed_ffn, w_in, preferred_element_type=jnp.float32)
    gate_proj = gate_up[:, :hidden_units]
    up_proj = gate_up[:, hidden_units:]
    sigmoid_gate = jax.nn.sigmoid(gate_proj)
    activated = gate_proj * sigmoid_gate
    hidden = (activated * up_proj).astype(jnp.bfloat16)
    layer_out = (res_f + jnp.dot(hidden, w_down, preferred_element_type=jnp.float32)).astype(
        jnp.bfloat16
    )
    d_hidden = jnp.einsum("rd,fd->rf", grad_out, w_down, preferred_element_type=jnp.float32)
    d_gate = d_hidden * up_proj * sigmoid_gate * (1.0 + gate_proj * (1.0 - sigmoid_gate))
    d_up = d_hidden * activated
    d_both = jnp.concatenate([d_gate, d_up], axis=1).astype(jnp.bfloat16)
    d_normed_ffn = jnp.einsum("rf,df->rd", d_both, w_in, preferred_element_type=jnp.float32)
    scaled_ffn = d_normed_ffn * gain_ffn
    d_resid = (
        grad_out.astype(jnp.float32)
        + inv_ffn
        * (scaled_ffn - unit_ffn * jnp.mean(scaled_ffn * unit_ffn, axis=-1, keepdims=True))
    ).astype(jnp.bfloat16)
    d_attn_t = jnp.einsum("de,re->dr", w_out, d_resid, preferred_element_type=jnp.float32).astype(
        jnp.bfloat16
    )
    d_heads = jnp.broadcast_to(
        d_attn_t.reshape(HEADS, 1, head_dim, rows), (HEADS, slices, head_dim, rows)
    ).reshape(seq_size, head_dim, rows)
    grads = lax.dynamic_slice_in_dim(all_to_all(d_heads), my_slice * tiles_here, tiles_here, 0)

    share = width // seq_size
    grad_out_local = jnp.einsum("dr,re->de", attn_out_t, d_resid, preferred_element_type=jnp.float32)
    grad_in_local = jnp.einsum("rd,rf->df", normed_ffn, d_both, preferred_element_type=jnp.float32)
    grad_down_local = jnp.einsum("rf,rd->fd", hidden, grad_out, preferred_element_type=jnp.float32)
    down_blocks = grad_down_local.astype(jnp.bfloat16).reshape(seq_size, -1, share, width)
    bits = seq_size.bit_length() - 1
    outer = list(range(2, bits))
    one, one_left = as_bits(grad_in_local.astype(jnp.bfloat16).reshape(seq_size, share, -1))
    two, two_left = as_bits(
        jnp.concatenate(
            [grad_out_local.astype(jnp.bfloat16).reshape(seq_size, share, -1)]
            + [down_blocks[:, i] for i in range(down_blocks.shape[1])],
            axis=2,
        )
    )
    one, one_left = halve(one, one_left, 0)
    two, two_left = halve(two, two_left, 0)
    grads, one, two = lax.optimization_barrier((grads, one, two))
    one, one_left = halve(one, one_left, 1)
    two, two_left = halve(two, two_left, outer[0])
    one_order = outer
    two_order = outer[1:] + [1]

    dq, dkv, dvirt = attention_backward(lists, qkv_all, virt, grads, head_dim)
    dq, one, two = lax.optimization_barrier((dq, one, two))
    virt_rows = 2 * head_dim * parts // rows
    back_send = jnp.concatenate(
        [
            spread(dq),
            dkv,
            jnp.broadcast_to(
                dvirt.astype(jnp.bfloat16).reshape(virt_rows, rows), (seq_size, virt_rows, rows)
            ),
        ],
        axis=1,
    )
    back = all_to_all(back_send)
    dq_t = pick_slice(back[:, :head_dim])
    rest = back[:, head_dim:]
    if slices > 1:
        rest = jnp.sum(
            rest.reshape(HEADS, slices, -1, rows).astype(jnp.float32), axis=1
        ).astype(jnp.bfloat16)
    d_qkv_t = jnp.concatenate(
        [dq_t, rest[:, :head_dim], rest[:, head_dim : 2 * head_dim]], axis=0
    ).reshape(3 * width, rows)
    d_virt = (
        rest[:, 2 * head_dim :]
        .reshape(HEADS, 2, head_dim, parts)
        .transpose(1, 0, 2, 3)
        .reshape(2 * width, parts)
    )
    d_virtual = jnp.einsum(
        "sp,ds->pd", d_virt, query_key_value_weight[:, width:], preferred_element_type=jnp.float32
    )
    inner_vn = jnp.mean(d_virtual * unit_vn, axis=-1, keepdims=True)
    per_part = inv_vn * (d_virtual - unit_vn * inner_vn) / counts
    grad_qkv_local = jnp.einsum("rd,cr->dc", normed, d_qkv_t, preferred_element_type=jnp.float32)
    late = grad_qkv_local.astype(jnp.bfloat16).reshape(seq_size, share, -1)
    for bit in one_order[:-1]:
        one, one_left = halve(one, one_left, bit, late)
    for bit in two_order[:-1]:
        two, two_left = halve(two, two_left, bit, late)
    d_normed = jnp.einsum(
        "cr,dc->rd", d_qkv_t, query_key_value_weight, preferred_element_type=jnp.float32
    )
    d_normed = d_normed + jnp.dot(member.astype(jnp.float32), per_part, precision=HIGH_PRECISION)
    scaled_attn = d_normed * gain_attn
    d_features = (
        d_resid.astype(jnp.float32)
        + inv_attn
        * (scaled_attn - unit_attn * jnp.mean(scaled_attn * unit_attn, axis=-1, keepdims=True))
    ).astype(jnp.bfloat16)
    gain_local = jnp.concatenate(
        [jnp.sum(d_normed * unit_attn, axis=0), jnp.sum(d_normed_ffn * unit_ffn, axis=0)]
    )
    gain_share = 2 * width // seq_size
    gain_block = jnp.pad(
        gain_local.astype(jnp.bfloat16).reshape(seq_size, 1, gain_share),
        ((0, 0), (0, share - 1), (0, 128 - gain_share)),
    )
    middle = late.shape[2] // 2
    late_one = late[:, :, :middle]
    late_two = jnp.concatenate([late[:, :, middle:], gain_block], axis=2)
    late_one, first_left = as_bits(late_one)
    late_two, second_left = as_bits(late_two)
    if share % 16 == 0:
        late_one, late_two, one, two = fold(
            [late_one, late_two, one, two],
            [[0, 1] + outer, [0] + outer + [1], one_left, two_left],
            bits,
        )
    else:
        one, one_left = halve(one, one_left, one_left[0])
        two, two_left = halve(two, two_left, two_left[0])
        for bit in [0, 1] + outer:
            late_one, first_left = halve(late_one, first_left, bit)
            late_two, second_left = halve(late_two, second_left, bit)
    late_sum = jnp.concatenate([late_one, late_two], axis=1)
    grad_gains = late_sum[0, 3 * width : 3 * width + gain_share]
    grad_w_in = one
    grad_w_out = two[:, :width]
    grad_w_down = jnp.concatenate(
        [two[:, c : c + width] for c in range(width, two.shape[1], width)], axis=0
    )
    my_virtual = lax.dynamic_slice_in_dim(virtual, me * share, share, 1)
    virtual_grad = jnp.einsum("pd,sp->ds", my_virtual, d_virt, preferred_element_type=jnp.float32)
    grad_qkv = jnp.concatenate(
        [late_sum[:, :width], late_sum[:, width : 3 * width] + virtual_grad], axis=1
    )
    return (layer_out, d_features, grad_qkv, grad_w_out, grad_w_in, grad_w_down, grad_gains)


def solution(mesh):
    node = P(("groups", "seq"), None)
    flat = P(("groups", "seq"))
    return jax.shard_map(
        on_device,
        mesh=mesh,
        in_specs=(node, P(), P(), P(), P(), P(), P(), node, flat, flat, node),
        out_specs=(node, node, node, node, node, node, flat),
        check_vma=False,
    )
```
